128 devices in a mesh: src: 4 (over z_lo, core), tile: 32 (over y, z_hi, x).
Axes of the slice: x: 4, y: 4, z: 4 (z_hi: 2, z_lo: 2; z = z_hi * 2 + z_lo), core: 2. Of those that a mesh axis runs over, the one named last changes fastest.
Arguments:
- mask_ids: int32 [4096, 4096], P(('src', 'tile')), may hold values from 0 to 3
- trans_table: float32 [2, 4], replicated, may hold values from -1 to 1
- pupil: float32 [2, 640, 640], replicated, may hold values from -1 to 1, as said below
- shifts: int32 [4, 2], P('src'), may hold values from -64 to 64
- weights: float32 [4], P('src'), may hold values from 0.03 to 0.12
- dose: float32 [2, 4096, 4096], P(None, 'tile', 'src'), may hold values from 2 to 8
- quencher: float32 [2], replicated, may hold values from 0.1 to 0.4
Outputs:
- acid: float32 [2, 4096, 4096], P(None, 'tile', 'src')
- inhibitor: float32 [2, 4096, 4096], P(None, 'tile', 'src')
The draws below stay inside these ranges and needn't reach their ends.
Inputs may be any that keep to these rules, and one draw needn't show every extreme that they name: `pupil`: zero outside the disc of radius 512//2 - 64 around index 320 in both dimensions, complex magnitude at most 1 inside.
All inputs are finite; a program needn't handle non-finite values.
Results may differ from the reference program's by a relative error of at most 0.0028.
The reference program's roundings to bfloat16 on the way count: a program that leaves them out, or rounds other values in their place, can miss the bound.
Values may be sent and summed in bfloat16 or wider, within the bound.
No kernel may reach another device: no remote copies, remote signals or barrier semaphores. Data moves between devices by JAX's collectives and lax.ppermute only.
A program may use at most 128 MiB of HBM per device.

```python
import math
import jax
import jax.numpy as jnp
from jax import lax

NPIX = 4096
PASS = 512
SHIFT = 64
LEVELS = 4
Z = 2
BAKE = 4
SOURCES = 4
PUP = 640


def draw_pupil(key, part):
    first_key, second_key = jax.random.split(key)
    offsets = jnp.arange(PUP, dtype=jnp.int32) - PUP // 2
    radius_sq = offsets[:, None] * offsets[:, None] + offsets[None, :] * offsets[None, :]
    radius = PASS // 2 - SHIFT
    inside = radius_sq <= radius * radius
    amplitude = jax.random.uniform(first_key, (PUP, PUP), jnp.float32, 0.5, 1.0)
    phase = jax.random.uniform(second_key, (PUP, PUP), jnp.float32, -math.pi, math.pi)
    real_part = jnp.where(inside, amplitude * jnp.cos(phase), 0.0)
    imag_part = jnp.where(inside, amplitude * jnp.sin(phase), 0.0)
    return jnp.stack([real_part, imag_part]).astype(jnp.float32)


def touch_ends(drawn, own_key, least, high):
    longest = drawn.shape.index(max(drawn.shape))
    spots = []
    for shift in (0, 1):
        where = [jax.random.randint(jax.random.fold_in(own_key, axis), (), 0, length) for axis, length in enumerate(drawn.shape)]
        where[longest] = (where[longest] + shift) % drawn.shape[longest]
        spots.append(tuple(where))
    return drawn.at[spots[0]].set(least).at[spots[1]].set(high)


def shard_levels(rng, dims, pieces, least, high):
    factor_of, own = 1.0, jax.random.fold_in(rng, 6)
    for axis_at, blocks in pieces:
        heights = jnp.exp(jax.random.uniform(jax.random.fold_in(own, axis_at), (blocks,), jnp.float32, least / len(pieces), high / len(pieces)))
        factor_of = factor_of * jnp.repeat(heights, dims[axis_at] // blocks).reshape([-1 if axis == axis_at else 1 for axis in range(len(dims))])
    return factor_of


def setup_inputs(seed: int = 0) -> dict:
    splits = jax.random.split(jax.random.key(seed), 8)
    mask_ids = touch_ends(jax.random.randint(splits[0], (NPIX, NPIX), 0, LEVELS), jax.random.fold_in(splits[0], 1), 0, LEVELS - 1).astype(jnp.int32)
    trans_table = jnp.clip(jax.random.uniform(splits[1], (2, LEVELS), jnp.float32, -1.0, 1.0), -1.0, 1.0)
    pupil = draw_pupil(jax.random.fold_in(splits[7], 71), 0)
    shifts = touch_ends(jax.random.randint(splits[3], (SOURCES, 2), -SHIFT, SHIFT + 1), jax.random.fold_in(splits[3], 1), -SHIFT, SHIFT).astype(jnp.int32)
    weights = jnp.clip(jnp.exp(math.log(0.12) - 1.3862944 * jax.random.uniform(splits[4], (SOURCES,), jnp.float32) ** shard_levels(splits[4], (SOURCES,), ((0, 4),), -0.2, 0.2)), 0.03, 0.12)
    dose = jnp.clip(jnp.exp(math.log(8.0) - 1.3862944 * jax.random.uniform(splits[5], (Z, NPIX, NPIX), jnp.float32) ** shard_levels(splits[5], (Z, NPIX, NPIX), ((1, 32), (2, 4)), -0.2, 0.2)), 2.0, 8.0)
    quencher = jnp.clip(jax.random.uniform(splits[6], (Z,), jnp.float32, 0.1, 0.4), 0.1, 0.4)
    return {"mask_ids": mask_ids, "trans_table": trans_table, "pupil": pupil, "shifts": shifts, "weights": weights, "dose": dose, "quencher": quencher}


DIFF_ACID = 0.12
DIFF_QUENCH = 0.04
QUENCH_RATE = 0.6
CATALYSIS = 0.4


def phase_tables(first_index, second_index, npix):
    product = jnp.mod(first_index[:, None] * second_index[None, :], npix)
    theta = product.astype(jnp.float32) * (2.0 * math.pi / npix)
    return jnp.cos(theta), jnp.sin(theta)


def band_freqs():
    return jnp.arange(PASS, dtype=jnp.int32) - PASS // 2


def transmission_planes(mask_ids, trans_table):
    real_part = jnp.zeros(mask_ids.shape, jnp.float32)
    imag_part = jnp.zeros(mask_ids.shape, jnp.float32)
    for level in range(LEVELS):
        hit = mask_ids == level
        real_part = jnp.where(hit, trans_table[0, level], real_part)
        imag_part = jnp.where(hit, trans_table[1, level], imag_part)
    return real_part.astype(jnp.bfloat16), imag_part.astype(jnp.bfloat16)


def forward_table():
    pixels = jnp.arange(NPIX, dtype=jnp.int32)
    cosine, sine = phase_tables(pixels, band_freqs(), NPIX)
    return jnp.concatenate([cosine, -sine], axis=1).astype(jnp.bfloat16)


def inverse_table(col_start, col_count):
    pixels = col_start + jnp.arange(col_count, dtype=jnp.int32)
    cosine, sine = phase_tables(band_freqs(), pixels, NPIX)
    return jnp.concatenate([cosine, sine], axis=1).astype(jnp.bfloat16)


def column_spectrum(trans_real, trans_imag, forward):
    first = jnp.dot(trans_real, forward, preferred_element_type=jnp.float32)
    second = jnp.dot(trans_imag, forward, preferred_element_type=jnp.float32)
    real_part = first[:, :PASS] - second[:, PASS:]
    imag_part = first[:, PASS:] + second[:, :PASS]
    return jnp.concatenate([real_part, imag_part], axis=1).astype(jnp.bfloat16)


def row_terms(piece, start):
    pixels = start + jnp.arange(piece.shape[0], dtype=jnp.int32)
    cosine, sine = phase_tables(band_freqs(), pixels, NPIX)
    first = jnp.dot(cosine.astype(jnp.bfloat16), piece, preferred_element_type=jnp.float32)
    second = jnp.dot(sine.astype(jnp.bfloat16), piece, preferred_element_type=jnp.float32)
    real_part = first[:, :PASS] + second[:, PASS:]
    imag_part = first[:, PASS:] - second[:, :PASS]
    return real_part, imag_part


def source_intensity(spec_real, spec_imag, pupil, shift, row_start, row_count, inverse):
    start_row = SHIFT - shift[0]
    start_col = SHIFT - shift[1]
    window = lax.dynamic_slice(pupil, (jnp.zeros((), jnp.int32), start_row, start_col), (2, PASS, PASS))
    filt_real = window[0] * spec_real - window[1] * spec_imag
    filt_imag = window[0] * spec_imag + window[1] * spec_real
    stacked = jnp.concatenate([filt_real, filt_imag], axis=1).astype(jnp.bfloat16)
    pixels = row_start + jnp.arange(row_count, dtype=jnp.int32)
    cosine, sine = phase_tables(pixels, band_freqs(), NPIX)
    first = jnp.dot(cosine.astype(jnp.bfloat16), stacked, preferred_element_type=jnp.float32)
    second = jnp.dot(sine.astype(jnp.bfloat16), stacked, preferred_element_type=jnp.float32)
    rows_real = (first[:, :PASS] - second[:, PASS:]).astype(jnp.bfloat16)
    rows_imag = (first[:, PASS:] + second[:, :PASS]).astype(jnp.bfloat16)
    upper = jnp.dot(rows_real, inverse, preferred_element_type=jnp.float32)
    lower = jnp.dot(rows_imag, inverse, preferred_element_type=jnp.float32)
    width = inverse.shape[1] // 2
    field_real = upper[:, :width] - lower[:, width:]
    field_imag = upper[:, width:] + lower[:, :width]
    return field_real * field_real + field_imag * field_imag


def bake_once(padded):
    center = padded[:, :, 1:-1, 1:-1]
    above = jnp.concatenate([center[:, 1:], center[:, -1:]], axis=1)
    below = jnp.concatenate([center[:, :1], center[:, :-1]], axis=1)
    lap = padded[:, :, 2:, 1:-1] + padded[:, :, :-2, 1:-1] + padded[:, :, 1:-1, 2:] + padded[:, :, 1:-1, :-2] + above + below - 6.0 * center
    acid_old = center[0]
    quench_old = center[1]
    reaction = QUENCH_RATE * acid_old * quench_old
    acid_new = acid_old + DIFF_ACID * lap[0] - reaction
    quench_new = quench_old + DIFF_QUENCH * lap[1] - reaction
    return jnp.stack([acid_new, quench_new]), acid_old


def reference(mask_ids, trans_table, pupil, shifts, weights, dose, quencher):
    trans_real, trans_imag = transmission_planes(mask_ids, trans_table)
    columns = column_spectrum(trans_real, trans_imag, forward_table())
    spec_real, spec_imag = row_terms(columns, jnp.zeros((), jnp.int32))
    scale = 1.0 / (NPIX * NPIX)
    spec_real = spec_real * scale
    spec_imag = spec_imag * scale
    inverse = inverse_table(jnp.zeros((), jnp.int32), NPIX)
    intensity = jnp.zeros((NPIX, NPIX), jnp.float32)
    for source in range(SOURCES):
        intensity = intensity + weights[source] * source_intensity(spec_real, spec_imag, pupil, shifts[source], jnp.zeros((), jnp.int32), NPIX, inverse)
    acid = 1.0 - jnp.exp(-dose * intensity[None])
    quench = jnp.broadcast_to(quencher[:, None, None], acid.shape)
    fields = jnp.stack([acid, quench])
    inhibitor = jnp.ones_like(acid)
    for step in range(BAKE):
        padded = jnp.pad(fields, ((0, 0), (0, 0), (1, 1), (1, 1)), mode="wrap")
        fields, before = bake_once(padded)
        inhibitor = inhibitor * jnp.exp(-CATALYSIS * before)
    return fields[0], inhibitor
```

```python
import math

import jax
import jax.numpy as jnp
import numpy as np
from jax import lax
from jax.experimental import pallas as pl
from jax.experimental.pallas import tpu as pltpu
from jax.sharding import Mesh, PartitionSpec as P

NPIX = 4096
PASS = 512
SHIFT = 64
LEVELS = 4
SOURCES = 4
BAKE = 4
Z = 2
DIFF_ACID = 0.12
DIFF_QUENCH = 0.04
QUENCH_RATE = 0.6
CATALYSIS = 0.4

DEVICES = 128
ROWS = NPIX // DEVICES
OWNERS = 32
FREQS = PASS // OWNERS
WIDE = 2 * FREQS
HALO = 4
TALL = 144
BRICK_ROWS = 128
BRICK_COLS = 1024
EXT_ROWS = BRICK_ROWS + 2 * HALO
EXT_COLS = BRICK_COLS + 128
COL_TILES = EXT_COLS // 128
ALL = ("zl", "c", "y", "zh", "x")
MIB = 1024 * 1024


def cos_sin(first, second):
    theta = (np.mod(first[:, None] * second[None, :], NPIX)).astype(np.float32)
    theta = (theta * np.float32(2.0 * math.pi / NPIX)).astype(np.float64)
    return np.cos(theta).astype(np.float32), np.sin(theta).astype(np.float32)


def bf16(table):
    return table.astype(jnp.bfloat16)


FREQ = np.arange(PASS, dtype=np.int64) - PASS // 2


def forward_columns():
    cosine, sine = cos_sin(np.arange(NPIX), FREQ)
    cosine = cosine.reshape(NPIX, OWNERS, 1, FREQS)
    sine = sine.reshape(NPIX, OWNERS, 1, FREQS)
    return bf16(np.concatenate([cosine, sine], axis=2).reshape(NPIX, 2 * PASS))


def forward_rows():
    order = np.arange(NPIX).reshape(DEVICES, 4, 8).transpose(1, 0, 2).reshape(NPIX)
    cosine, sine = cos_sin(FREQ, order)
    both = np.concatenate([cosine, sine], axis=0)
    return bf16(both.reshape(2 * PASS, 4, NPIX // 4).transpose(1, 0, 2))


def inverse_rows(tiles):
    blocks = []
    for tile in range(tiles):
        pixels = np.mod(tile * BRICK_ROWS - HALO + np.arange(TALL), NPIX)
        cosine, sine = cos_sin(pixels, FREQ)
        upper = np.concatenate([cosine, -sine], axis=1)
        lower = np.concatenate([sine, cosine], axis=1)
        blocks.append(np.concatenate([upper, lower], axis=0))
    return bf16(np.stack(blocks))


def inverse_cols(sources):
    lanes = np.arange(EXT_COLS)
    local = np.where(lanes < BRICK_COLS + 64, lanes, lanes - EXT_COLS)
    blocks = []
    for source in range(sources):
        pixels = np.mod(source * BRICK_COLS + local, NPIX)
        cosine, sine = cos_sin(FREQ, pixels)
        real = np.concatenate([cosine, -sine], axis=0).reshape(2 * PASS, COL_TILES, 1, 128)
        imag = np.concatenate([sine, cosine], axis=0).reshape(2 * PASS, COL_TILES, 1, 128)
        both = np.concatenate([real, imag], axis=2).reshape(2 * PASS, COL_TILES, 256)
        blocks.append(both.transpose(1, 0, 2))
    return bf16(np.stack(blocks))


def lane_ids(shape):
    return lax.broadcasted_iota(jnp.int32, shape, len(shape) - 1)


def columns_kernel(trans_ref, ids_ref, table_ref, out_ref, acc_ref):
    step = pl.program_id(0)
    ids = ids_ref[...]
    parts = []
    for plane in range(2):
        value = jnp.zeros(ids.shape, jnp.float32)
        for level in range(LEVELS):
            value = jnp.where(ids == level, trans_ref[plane, level], value)
        parts.append(value)
    trans = jnp.concatenate(parts, axis=0).astype(jnp.bfloat16)
    product = jnp.dot(trans, table_ref[...], preferred_element_type=jnp.float32)

    @pl.when(step == 0)
    def _():
        acc_ref[...] = product

    @pl.when(step > 0)
    def _():
        acc_ref[...] += product

    @pl.when(step == pl.num_programs(0) - 1)
    def _():
        upper = acc_ref[:ROWS, :]
        lower = acc_ref[ROWS:, :]
        width = upper.shape[1]
        is_real = lane_ids(upper.shape) % WIDE < FREQS
        columns = jnp.where(
            is_real,
            upper + pltpu.roll(lower, width - FREQS, 1),
            pltpu.roll(lower, FREQS, 1) - upper,
        )
        group = lane_ids((8, 128)) // WIDE
        chunks = []
        for owner in range(OWNERS):
            major, minor = owner // 4, owner % 4
            chunk = jnp.zeros((8, 128), jnp.float32)
            for q in range(4):
                piece = columns[8 * q : 8 * q + 8, 128 * major : 128 * major + 128]
                turn = (q - minor) % 4 * WIDE
                piece = pltpu.roll(piece, turn, 1) if turn else piece
                chunk = jnp.where(group == q, piece, chunk)
            chunks.append(chunk)
        for pair in range(DEVICES // 2):
            both = []
            for dest in (2 * pair, 2 * pair + 1):
                core, y, x = dest // 32 % 2, dest // 8 % 4, dest % 4
                both.append(chunks[core * 16 + y * 4 + x])
            out_ref[16 * pair : 16 * pair + 16, :] = jnp.concatenate(both, axis=0).astype(jnp.bfloat16)


def columns_call(trans_table, mask_ids, table):
    steps = 4
    depth = NPIX // steps
    return pl.pallas_call(
        columns_kernel,
        grid=(steps,),
        out_shape=jax.ShapeDtypeStruct((DEVICES * 8, 128), jnp.bfloat16),
        in_specs=[
            pl.BlockSpec(memory_space=pltpu.SMEM),
            pl.BlockSpec((ROWS, depth), lambda k: (0, k)),
            pl.BlockSpec((depth, 2 * PASS), lambda k: (k, 0)),
        ],
        out_specs=pl.BlockSpec((DEVICES * 8, 128), lambda k: (0, 0)),
        scratch_shapes=[pltpu.VMEM((2 * ROWS, 2 * PASS), jnp.float32)],
        compiler_params=pltpu.CompilerParams(vmem_limit_bytes=20 * MIB),
        name="columns",
    )(trans_table, mask_ids, table)


def spectrum_kernel(table_ref, cols_ref, out_ref, acc_ref):
    step = pl.program_id(0)
    product = jnp.dot(table_ref[0], cols_ref[...], preferred_element_type=jnp.float32)
    group = lane_ids(product.shape) // WIDE

    @pl.when(step == 0)
    def _():
        acc_ref[...] = product

    @pl.when(step > 0)
    def _():
        acc_ref[...] = jnp.where(group == step, product, acc_ref[...])

    @pl.when(step == pl.num_programs(0) - 1)
    def _():
        total = acc_ref[...]
        total = total + pltpu.roll(total, 64, 1)
        total = total + pltpu.roll(total, 32, 1)
        cosine, sine = total[:PASS], total[PASS:]
        is_real = lane_ids(cosine.shape) % WIDE < FREQS
        turned = jnp.where(is_real, pltpu.roll(sine, 128 - FREQS, 1), -pltpu.roll(sine, FREQS, 1))
        spectrum = (cosine + turned) * (1.0 / (NPIX * NPIX))
        block = jnp.transpose(spectrum)[:WIDE, :]
        for dest in range(16):
            out_ref[dest * WIDE : (dest + 1) * WIDE, :] = block


def spectrum_call(table, cols):
    return pl.pallas_call(
        spectrum_kernel,
        grid=(4,),
        out_shape=jax.ShapeDtypeStruct((16 * WIDE, PASS), jnp.float32),
        in_specs=[
            pl.BlockSpec((1, 2 * PASS, NPIX // 4), lambda q: (q, 0, 0)),
            pl.BlockSpec((NPIX // 4, 128), lambda q: (0, 0)),
        ],
        out_specs=pl.BlockSpec((16 * WIDE, PASS), lambda q: (0, 0)),
        scratch_shapes=[pltpu.VMEM((2 * PASS, 128), jnp.float32)],
        compiler_params=pltpu.CompilerParams(vmem_limit_bytes=20 * MIB),
        name="spectrum",
    )(table, cols)


def resist_kernel(
    core_ref, weights_ref, quencher_ref, own_ref, other_ref, window_ref, rows_ref, cols_ref, dose_ref,
    acid_ref, inhibitor_ref, filt_ref, field_ref, a_ref, b_ref, p_ref, q_ref, sum_ref,
):
    core = core_ref[0]

    def source_step(s, carry):
        def filter_from(spec_ref, half):
            def block(o, inner):
                row = pl.multiple_of(half * (PASS // 2) + o * FREQS, FREQS)
                base = pl.multiple_of(o * WIDE, WIDE)
                real = spec_ref[pl.ds(base, FREQS), :]
                imag = spec_ref[pl.ds(base + FREQS, FREQS), :]
                w_real = window_ref[2 * s, pl.ds(row, FREQS), :]
                w_imag = window_ref[2 * s + 1, pl.ds(row, FREQS), :]
                filt_ref[pl.ds(row, FREQS), :PASS] = (w_real * real - w_imag * imag).astype(jnp.bfloat16)
                filt_ref[pl.ds(row, FREQS), PASS:] = (w_real * imag + w_imag * real).astype(jnp.bfloat16)
                return inner

            lax.fori_loop(0, 16, block, 0, unroll=4)

        filter_from(own_ref, core)
        filter_from(other_ref, 1 - core)
        rowfield = lax.dot_general(
            rows_ref[...], filt_ref[...], (((1,), (1,)), ((), ())), preferred_element_type=jnp.float32
        ).astype(jnp.bfloat16)
        top = pl.multiple_of(s * TALL, 16)
        field_ref[pl.ds(top, TALL), :PASS] = rowfield[:TALL]
        field_ref[pl.ds(top, TALL), PASS:] = rowfield[TALL:]
        return carry

    lax.fori_loop(0, SOURCES, source_step, 0)

    def tile_step(b, carry):
        field = jnp.dot(field_ref[...], cols_ref[b], preferred_element_type=jnp.float32)
        intensity = jnp.zeros((EXT_ROWS, 128), jnp.float32)
        for s in range(SOURCES):
            part = field[s * TALL : s * TALL + EXT_ROWS]
            real, imag = part[:, :128], part[:, 128:]
            intensity = intensity + weights_ref[s] * (real * real + imag * imag)
        lanes = pl.ds(pl.multiple_of(b * 128, 128), 128)
        for z in range(Z):
            a_ref[z, :, lanes] = 1.0 - jnp.exp(-dose_ref[z, :, lanes] * intensity)
        return carry

    lax.fori_loop(0, COL_TILES, tile_step, 0)

    tiles = EXT_ROWS // 8
    row_id = lax.broadcasted_iota(jnp.int32, (8, EXT_COLS), 0)
    quench = [quencher_ref[0], quencher_ref[1]]

    def neighbours(ref, z, t):
        here = ref[z, pl.ds(pl.multiple_of(t * 8, 8), 8), :]
        before = ref[z, pl.ds(pl.multiple_of(jnp.maximum(t - 1, 0) * 8, 8), 8), :]
        after = ref[z, pl.ds(pl.multiple_of(jnp.minimum(t + 1, tiles - 1) * 8, 8), 8), :]
        above = pltpu.roll(jnp.where(row_id == 7, before, here), 1, 0)
        below = pltpu.roll(jnp.where(row_id == 0, after, here), 7, 0)
        left = pltpu.roll(here, 1, 1)
        right = pltpu.roll(here, EXT_COLS - 1, 1)
        return here, (above + below) + (left + right)

    buffers = [(a_ref, b_ref), (b_ref, a_ref), (a_ref, b_ref), (b_ref, a_ref)]
    quenches = [(None, p_ref), (p_ref, q_ref), (q_ref, p_ref), (p_ref, None)]
    for step in range(BAKE):
        old, new = buffers[step]
        q_old, q_new = quenches[step]

        def row_step(t, carry):
            rows = pl.ds(pl.multiple_of(t * 8, 8), 8)
            acid = [neighbours(old, z, t) for z in range(Z)]
            acid_z = acid[0][0] + acid[1][0]
            if q_old is None:
                quench_here = quench
                quench_sum = [4.0 * quench[z] for z in range(Z)]
            elif q_new is None:
                quench_here = [q_old[z, rows, :] for z in range(Z)]
            else:
                pairs = [neighbours(q_old, z, t) for z in range(Z)]
                quench_here = [pair[0] for pair in pairs]
                quench_sum = [pair[1] for pair in pairs]
            quench_z = quench_here[0] + quench_here[1]
            for z in range(Z):
                here, around = acid[z]
                reaction = QUENCH_RATE * here * quench_here[z]
                lap = (around + acid_z) - 6.0 * here
                new[z, rows, :] = here + DIFF_ACID * lap - reaction
                if q_new is not None:
                    q_lap = (quench_sum[z] + quench_z) - 6.0 * quench_here[z]
                    q_new[z, rows, :] = quench_here[z] + DIFF_QUENCH * q_lap - reaction
                if step == 0:
                    sum_ref[z, rows, :] = here[:, :BRICK_COLS]
                else:
                    sum_ref[z, rows, :] = sum_ref[z, rows, :] + here[:, :BRICK_COLS]
            return carry

        lax.fori_loop(0, tiles, row_step, 0)

    for z in range(Z):
        acid_ref[z] = a_ref[z, HALO : HALO + BRICK_ROWS, :BRICK_COLS]
        inhibitor_ref[z] = jnp.exp(-CATALYSIS * sum_ref[z, HALO : HALO + BRICK_ROWS, :])


def resist_call(core, weights, quencher, own, other, window, rows, cols, dose):
    smem = pl.BlockSpec(memory_space=pltpu.SMEM)
    vmem = pl.BlockSpec(memory_space=pltpu.VMEM)
    out = jax.ShapeDtypeStruct((Z, BRICK_ROWS, BRICK_COLS), jnp.float32)
    brick = pltpu.VMEM((Z, EXT_ROWS, EXT_COLS), jnp.float32)
    return pl.pallas_call(
        resist_kernel,
        out_shape=(out, out),
        in_specs=[smem, smem, smem] + [vmem] * 6,
        out_specs=(vmem, vmem),
        scratch_shapes=[
            pltpu.VMEM((PASS, 2 * PASS), jnp.bfloat16),
            pltpu.VMEM((SOURCES * TALL, 2 * PASS), jnp.bfloat16),
            brick, brick, brick, brick,
            pltpu.VMEM((Z, EXT_ROWS, BRICK_COLS), jnp.float32),
        ],
        compiler_params=pltpu.CompilerParams(vmem_limit_bytes=40 * MIB),
        name="resist",
    )(core, weights, quencher, own, other, window, rows, cols, dose)


def ring(axes, step):
    size = lax.axis_size(axes)
    return [(i, (i + step) % size) for i in range(size)]


def extend_dose(dose):
    src, tile = ("zl", "c"), ("y", "zh", "x")
    left = lax.ppermute(dose[:, :, BRICK_COLS - HALO :], src, ring(src, 1))
    right = lax.ppermute(dose[:, :, :HALO], src, ring(src, -1))
    middle = jnp.zeros((Z, BRICK_ROWS, EXT_COLS - BRICK_COLS - 2 * HALO), dose.dtype)
    wide = jnp.concatenate([dose, right, middle, left], axis=2)
    above = lax.ppermute(wide[:, BRICK_ROWS - HALO :], tile, ring(tile, 1))
    below = lax.ppermute(wide[:, :HALO], tile, ring(tile, -1))
    return jnp.concatenate([above, wide, below], axis=1)


def gather_sources(shifts, weights):
    src = ("zl", "c")
    mine = jnp.concatenate([shifts[0].astype(jnp.float32), weights])
    me = lax.axis_index(src)
    rows = [mine]
    for step in (1, 2, 3):
        rows.append(lax.ppermute(mine, src, [(i, i ^ step) for i in range(4)]))
    stacked = jnp.stack(rows)
    order = jnp.bitwise_xor(jnp.arange(SOURCES), me)
    picked = sum(jnp.where((order == k)[:, None], stacked[k][None], 0.0) for k in range(SOURCES))
    return picked[:, :2].astype(jnp.int32), picked[:, 2]


def body(mask_ids, trans_table, pupil, shifts, weights, dose, quencher):
    src = lax.axis_index(("zl", "c"))
    tile = lax.axis_index(("y", "zh", "x"))
    packed = columns_call(trans_table, mask_ids, jnp.asarray(forward_columns()))
    cols = lax.all_to_all(packed, ALL, 0, 0, tiled=True)

    all_shifts, all_weights = gather_sources(shifts, weights)
    flipped = jnp.transpose(pupil, (0, 2, 1))
    zero = jnp.zeros((), jnp.int32)
    windows = [
        lax.dynamic_slice(flipped, (zero, SHIFT - all_shifts[s, 1], SHIFT - all_shifts[s, 0]), (2, PASS, PASS))
        for s in range(SOURCES)
    ]
    window = jnp.concatenate(windows, axis=0)
    dose_ext = extend_dose(dose)
    row_table = lax.dynamic_index_in_dim(jnp.asarray(inverse_rows(32)), tile, 0, keepdims=False)
    col_table = lax.dynamic_index_in_dim(jnp.asarray(inverse_cols(4)), src, 0, keepdims=False)

    block = spectrum_call(jnp.asarray(forward_rows()), cols)
    own = lax.all_to_all(block, ("y", "x"), 0, 0, tiled=True)
    other = lax.ppermute(own, "c", [(0, 1), (1, 0)])
    core = lax.axis_index("c").reshape(1).astype(jnp.int32)
    return resist_call(core, all_weights, quencher, own, other, window, row_table, col_table, dose_ext)


def solution(mesh):
    parts = Mesh(mesh.devices.reshape(2, 2, 4, 2, 4), ALL)
    src, tile = ("zl", "c"), ("y", "zh", "x")
    inner = jax.shard_map(
        body,
        mesh=parts,
        in_specs=(
            P(ALL, None),
            P(),
            P(),
            P(src, None),
            P(src),
            P(None, tile, src),
            P(),
        ),
        out_specs=(P(None, tile, src), P(None, tile, src)),
        check_vma=False,
    )
    return inner
```

```python
import math

import jax
import jax.numpy as jnp
import numpy as np
from jax import lax
from jax.experimental import pallas as pl
from jax.experimental.pallas import tpu as pltpu
from jax.sharding import Mesh, PartitionSpec as P

NPIX = 4096
PASS = 512
SHIFT = 64
LEVELS = 4
SOURCES = 4
BAKE = 4
Z = 2
PUPIL_TILES = (PASS + 2 * SHIFT) // 8
DIFF_ACID = 0.12
DIFF_QUENCH = 0.04
QUENCH_RATE = 0.6
CATALYSIS = 0.4

DEVICES = 128
ROWS = NPIX // DEVICES
OWNERS = 32
FREQS = PASS // OWNERS
WIDE = 2 * FREQS
HALO = 4
TALL = 144
BRICK_ROWS = 128
BRICK_COLS = 1024
EXT_ROWS = BRICK_ROWS + 2 * HALO
EXT_COLS = BRICK_COLS + 128
COL_TILES = EXT_COLS // 128
ALL = ("zl", "c", "y", "zh", "x")
MIB = 1024 * 1024
FILTER_UNROLL = 16
FIELD_UNROLL = 9
BAKE_UNROLL = 17


def cos_sin(first, second):
    theta = (np.mod(first[:, None] * second[None, :], NPIX)).astype(np.float32)
    theta = (theta * np.float32(2.0 * math.pi / NPIX)).astype(np.float64)
    return np.cos(theta).astype(np.float32), np.sin(theta).astype(np.float32)


def bf16(table):
    return table.astype(jnp.bfloat16)


FREQ = np.arange(PASS, dtype=np.int64) - PASS // 2
HALF = PASS // 2


def forward_columns():
    return bf16(np.concatenate(cos_sin(np.arange(NPIX), np.arange(HALF)), axis=1))


def forward_rows():
    order = np.arange(NPIX).reshape(DEVICES, 4, 8).transpose(1, 0, 2).reshape(NPIX)
    both = np.concatenate(cos_sin(np.arange(HALF), order), axis=0)
    return bf16(both.reshape(PASS, 4, NPIX // 4).transpose(1, 0, 2))


def edge_columns():
    cosine, sine = cos_sin(np.array([HALF]), np.arange(128))
    return np.asarray(bf16(np.concatenate([cosine, sine], axis=0))).astype(np.float32)


def edge_rows():
    rows = np.arange(4)[None, :] * 8 + np.arange(8)[:, None]
    cosine, sine = cos_sin(np.array([HALF]), rows.reshape(-1))
    both = np.stack([cosine.reshape(8, 4), sine.reshape(8, 4)])
    return np.asarray(bf16(np.repeat(both, WIDE, axis=2))).astype(np.float32)


def inverse_rows(tiles):
    blocks = []
    for tile in range(tiles):
        local = np.arange(TALL)
        local = np.where(local < BRICK_ROWS + HALO, local, local - EXT_ROWS)
        pixels = np.mod(tile * BRICK_ROWS + local, NPIX)
        cosine, sine = cos_sin(pixels, FREQ)
        upper = np.concatenate([cosine, -sine], axis=1)
        lower = np.concatenate([sine, cosine], axis=1)
        blocks.append(np.concatenate([upper, lower], axis=0))
    return bf16(np.stack(blocks))


def inverse_cols(sources):
    lanes = np.arange(EXT_COLS)
    local = np.where(lanes < BRICK_COLS + 64, lanes, lanes - EXT_COLS)
    blocks = []
    for source in range(sources):
        pixels = np.mod(source * BRICK_COLS + local, NPIX)
        cosine, sine = cos_sin(FREQ, pixels)
        real = np.concatenate([cosine, -sine], axis=0).reshape(2 * PASS, COL_TILES, 1, 128)
        imag = np.concatenate([sine, cosine], axis=0).reshape(2 * PASS, COL_TILES, 1, 128)
        both = np.concatenate([real, imag], axis=2).reshape(2 * PASS, COL_TILES, 256)
        blocks.append(both.transpose(1, 0, 2))
    return bf16(np.stack(blocks))


def lane_ids(shape):
    return lax.broadcasted_iota(jnp.int32, shape, len(shape) - 1)


def columns_kernel(trans_ref, ids_ref, table_ref, edge_ref, out_ref, acc_ref, sum_ref, perm_ref):
    step = pl.program_id(0)

    @pl.when(step == 0)
    def _():
        acc_ref[...] = jnp.zeros_like(acc_ref)
        sum_ref[...] = jnp.zeros_like(sum_ref)
        source = lax.broadcasted_iota(jnp.int32, (PASS, PASS), 0)
        lane = lax.broadcasted_iota(jnp.int32, (PASS, PASS), 1)
        plane, place = lane // FREQS % 2, lane // WIDE * FREQS + lane % FREQS
        perm_ref[0] = (source == plane * HALF + (HALF - place) % HALF).astype(jnp.float32).astype(jnp.bfloat16)
        perm_ref[1] = (source == plane * HALF + place).astype(jnp.float32).astype(jnp.bfloat16)

    ids = ids_ref[...]
    parts = []
    for plane in range(2):
        value = jnp.zeros(ids.shape, jnp.float32)
        for level in range(LEVELS):
            value = jnp.where(ids == level, trans_ref[plane, level], value)
        parts.append(value)
    trans = jnp.concatenate(parts, axis=0).astype(jnp.bfloat16)
    acc_ref[...] += jnp.dot(trans, table_ref[...], preferred_element_type=jnp.float32)
    exact = trans.astype(jnp.float32)
    total = sum_ref[...]
    for tile in range(ids.shape[1] // 128):
        total = total + exact[:, 128 * tile : 128 * tile + 128]
    sum_ref[...] = total

    @pl.when(step == pl.num_programs(0) - 1)
    def _():
        edge_cos = jnp.sum(sum_ref[...] * edge_ref[0:1, :], axis=1, keepdims=True)
        edge_sin = jnp.sum(sum_ref[...] * edge_ref[1:2, :], axis=1, keepdims=True)
        cos_real, cos_imag = acc_ref[:ROWS, :HALF], acc_ref[ROWS:, :HALF]
        sin_real, sin_imag = acc_ref[:ROWS, HALF:], acc_ref[ROWS:, HALF:]
        first = lane_ids((ROWS, HALF)) == 0
        low_real = jnp.where(first, edge_cos[:ROWS] - edge_sin[ROWS:], cos_real - sin_imag)
        low_imag = jnp.where(first, edge_cos[ROWS:] + edge_sin[:ROWS], cos_imag + sin_real)
        low = jnp.concatenate([low_real, low_imag], axis=1).astype(jnp.bfloat16)
        high = jnp.concatenate([cos_real + sin_imag, cos_imag - sin_real], axis=1).astype(jnp.bfloat16)
        sides = [
            jnp.dot(low, perm_ref[0], preferred_element_type=jnp.float32),
            jnp.dot(high, perm_ref[1], preferred_element_type=jnp.float32),
        ]
        group = lane_ids((8, 128)) // WIDE
        chunks = []
        for owner in range(OWNERS):
            major, minor = owner % 16 // 4, owner % 4
            chunk = jnp.zeros((8, 128), jnp.float32)
            for q in range(4):
                piece = sides[owner // 16][8 * q : 8 * q + 8, 128 * major : 128 * major + 128]
                turn = (q - minor) % 4 * WIDE
                piece = pltpu.roll(piece, turn, 1) if turn else piece
                chunk = jnp.where(group == q, piece, chunk)
            chunks.append(chunk)
        for pair in range(DEVICES // 2):
            both = []
            for dest in (2 * pair, 2 * pair + 1):
                core, y, x = dest // 32 % 2, dest // 8 % 4, dest % 4
                both.append(chunks[core * 16 + y * 4 + x])
            out_ref[16 * pair : 16 * pair + 16, :] = jnp.concatenate(both, axis=0).astype(jnp.bfloat16)


def columns_call(trans_table, mask_ids, table, edge):
    steps = 4
    depth = NPIX // steps
    return pl.pallas_call(
        columns_kernel,
        grid=(steps,),
        out_shape=jax.ShapeDtypeStruct((DEVICES * 8, 128), jnp.bfloat16),
        in_specs=[
            pl.BlockSpec(memory_space=pltpu.SMEM),
            pl.BlockSpec((ROWS, depth), lambda k: (0, k)),
            pl.BlockSpec((depth, PASS), lambda k: (k, 0)),
            pl.BlockSpec((2, 128), lambda k: (0, 0)),
        ],
        out_specs=pl.BlockSpec((DEVICES * 8, 128), lambda k: (0, 0)),
        scratch_shapes=[
            pltpu.VMEM((2 * ROWS, PASS), jnp.float32),
            pltpu.VMEM((2 * ROWS, 128), jnp.float32),
            pltpu.VMEM((2, PASS, PASS), jnp.bfloat16),
        ],
        compiler_params=pltpu.CompilerParams(vmem_limit_bytes=56 * MIB),
        name="columns",
    )(trans_table, mask_ids, table, edge)


def spectrum_kernel(table_ref, cols_ref, edge_ref, out_ref, acc_ref):
    step = pl.program_id(0)
    product = jnp.dot(table_ref[0], cols_ref[...], preferred_element_type=jnp.float32)
    group = lane_ids(product.shape) // WIDE

    @pl.when(step == 0)
    def _():
        acc_ref[...] = product

    @pl.when(step > 0)
    def _():
        acc_ref[...] = jnp.where(group == step, product, acc_ref[...])

    @pl.when(step == pl.num_programs(0) - 1)
    def _():
        columns = cols_ref[...].astype(jnp.float32)
        total = [columns[16 * k : 16 * k + 16] for k in range(DEVICES // 2)]
        while len(total) > 1:
            total = [a + b for a, b in zip(total[::2], total[1::2])]
        total = total[0][:8] + total[0][8:]
        edge_cos = jnp.sum(total * edge_ref[0], axis=0, keepdims=True)
        edge_sin = jnp.sum(total * edge_ref[1], axis=0, keepdims=True)

        def fold(value):
            value = value + pltpu.roll(value, 64, 1)
            return value + pltpu.roll(value, 32, 1)

        def turn(value):
            is_real = lane_ids(value.shape) % WIDE < FREQS
            return jnp.where(is_real, pltpu.roll(value, 128 - FREQS, 1), -pltpu.roll(value, FREQS, 1))

        edges = fold(jnp.concatenate([edge_cos, edge_sin, jnp.zeros((6, 128), jnp.float32)], axis=0))
        edge = edges[0:1] - turn(edges)[1:2]
        folded = fold(acc_ref[...])
        cosine, turned = folded[:HALF], turn(folded[HALF:])
        first = lax.broadcasted_iota(jnp.int32, cosine.shape, 0) == 0
        scale = 1.0 / (NPIX * NPIX)
        high = jnp.transpose((cosine + turned) * scale)[:WIDE]
        low = jnp.transpose(jnp.where(first, edge, cosine - turned) * scale)[:WIDE]
        source = lax.broadcasted_iota(jnp.int32, (HALF, HALF), 0)
        place = lax.broadcasted_iota(jnp.int32, (HALF, HALF), 1)
        perm = (source == (HALF - place) % HALF).astype(jnp.float32).astype(jnp.bfloat16)
        pieces = []
        rest = low
        for _ in range(3):
            piece = rest.astype(jnp.bfloat16)
            rest = rest - piece.astype(jnp.float32)
            pieces.append(jnp.dot(piece, perm, preferred_element_type=jnp.float32))
        block = jnp.concatenate([pieces[0] + pieces[1] + pieces[2], high], axis=1)
        for dest in range(16):
            out_ref[dest * WIDE : (dest + 1) * WIDE, :] = block


def spectrum_call(table, cols, edge):
    return pl.pallas_call(
        spectrum_kernel,
        grid=(4,),
        out_shape=jax.ShapeDtypeStruct((16 * WIDE, PASS), jnp.float32),
        in_specs=[
            pl.BlockSpec((1, PASS, NPIX // 4), lambda q: (q, 0, 0)),
            pl.BlockSpec((NPIX // 4, 128), lambda q: (0, 0)),
            pl.BlockSpec((2, 8, 128), lambda q: (0, 0, 0)),
        ],
        out_specs=pl.BlockSpec((16 * WIDE, PASS), lambda q: (0, 0)),
        scratch_shapes=[pltpu.VMEM((PASS, 128), jnp.float32)],
        compiler_params=pltpu.CompilerParams(vmem_limit_bytes=56 * MIB),
        name="spectrum",
    )(table, cols, edge)


def pack_kernel(shifts_ref, weights_ref, pupil_ref, dose_ref, turned_ref, last_ref, first_ref, note_ref):
    blocks = pupil_ref.shape[1] // 128
    for plane in range(2):
        for i in range(blocks):
            for j in range(blocks):
                piece = pupil_ref[plane, 128 * i : 128 * i + 128, 128 * j : 128 * j + 128]
                turned_ref[plane, 128 * j : 128 * j + 128, 128 * i : 128 * i + 128] = jnp.transpose(piece)

    def note(shape):
        lane = lane_ids(shape)
        shift_x, shift_y = shifts_ref[0, 0].astype(jnp.float32), shifts_ref[0, 1].astype(jnp.float32)
        return jnp.where(lane == 64, shift_x, jnp.where(lane == 65, shift_y, weights_ref[0]))

    lane = lane_ids((BRICK_ROWS, 128))
    middle = (lane >= 64) & (lane < 67)
    for z in range(Z):
        last_ref[z] = jnp.where(middle, note((BRICK_ROWS, 128)), dose_ref[z, :, BRICK_COLS - 128 :])
        first_ref[z] = jnp.where(middle, note((BRICK_ROWS, 128)), dose_ref[z, :, :128])
    note_ref[...] = note((8, 128))


def pack_call(shifts, weights, pupil, dose):
    vmem = pl.BlockSpec(memory_space=pltpu.VMEM)
    smem = pl.BlockSpec(memory_space=pltpu.SMEM)
    side = jax.ShapeDtypeStruct((Z, BRICK_ROWS, 128), jnp.float32)
    return pl.pallas_call(
        pack_kernel,
        out_shape=(
            jax.ShapeDtypeStruct(pupil.shape, jnp.float32),
            side,
            side,
            jax.ShapeDtypeStruct((8, 128), jnp.float32),
        ),
        in_specs=[smem, smem, vmem, vmem],
        out_specs=(vmem,) * 4,
        compiler_params=pltpu.CompilerParams(vmem_limit_bytes=12 * MIB),
        cost_estimate=pl.CostEstimate(flops=1_000_000, bytes_accessed=9_000_000, transcendentals=0),
        name="pack",
    )(shifts, weights, pupil, dose)


def edge_kernel(dose_ref, before_ref, after_ref, side_ref, last_ref, first_ref):
    lane = lane_ids((BRICK_ROWS, 128))
    for z in range(Z):
        side = jnp.where(lane < 64, after_ref[z], before_ref[z])
        side_ref[z] = side
        last_ref[z, :, :BRICK_COLS] = dose_ref[z, BRICK_ROWS - 8 :, :]
        last_ref[z, :, BRICK_COLS:] = side[BRICK_ROWS - 8 :]
        first_ref[z, :, :BRICK_COLS] = dose_ref[z, :8, :]
        first_ref[z, :, BRICK_COLS:] = side[:8]


def edge_call(dose, before, after):
    vmem = pl.BlockSpec(memory_space=pltpu.VMEM)
    row = jax.ShapeDtypeStruct((Z, 8, EXT_COLS), jnp.float32)
    return pl.pallas_call(
        edge_kernel,
        out_shape=(jax.ShapeDtypeStruct((Z, BRICK_ROWS, 128), jnp.float32), row, row),
        in_specs=[vmem] * 3,
        out_specs=(vmem,) * 3,
        compiler_params=pltpu.CompilerParams(vmem_limit_bytes=6 * MIB),
        cost_estimate=pl.CostEstimate(flops=1_000_000, bytes_accessed=2_000_000, transcendentals=0),
        name="edge",
    )(dose, before, after)


def window_kernel(shifts_ref, turned_ref, dose_hbm, out_ref, dose_ref, sem):
    copy = pltpu.make_async_copy(dose_hbm, dose_ref, sem)
    copy.start()
    lane = lane_ids((8, 128))
    row = lax.broadcasted_iota(jnp.int32, (8, 128), 0)
    zero = jnp.zeros((8, 128), jnp.float32)
    tiles, group, groups = PASS // 8, 13, 4
    edge = SHIFT * 2 // 8

    def source_step(s, carry):
        lift = SHIFT - shifts_ref[s, 1]
        shift = SHIFT - shifts_ref[s, 0]
        first, rest = lift // 8, lax.rem(lift, 8)
        rise = lax.rem(8 - rest, 8)
        turn = lax.rem(256 - shift, 128)
        keep_lane = lane < 128 - shift
        keep_row = row < 8 - rest
        begin = jnp.minimum(edge - first - jnp.where(rest > 0, 1, 0), tiles - group * groups)

        def clear(t, inner):
            for plane in range(2):
                for v in range(4):
                    out_ref[2 * s + plane, pl.ds(pl.multiple_of(t * 8, 8), 8), 128 * v : 128 * v + 128] = zero
            return inner

        lax.fori_loop(0, begin, clear, 0)
        lax.fori_loop(begin + group * groups, tiles, clear, 0)

        def block(t, inner):
            start = begin + t * group
            for plane in range(2):
                before = None
                for k in range(group + 1):
                    tile = jnp.minimum(start + k + first, PUPIL_TILES - 1)
                    base = pl.ds(pl.multiple_of(tile * 8, 8), 8)
                    turned = [zero] + [
                        pltpu.roll(turned_ref[plane, base, 128 * v : 128 * v + 128], turn, 1) for v in range(1, 5)
                    ]
                    cut = [jnp.where(keep_lane, turned[v], turned[v + 1]) for v in range(4)]
                    after = [pltpu.roll(c, rise, 0) for c in cut]
                    if before is not None:
                        place = pl.ds(pl.multiple_of((start + k - 1) * 8, 8), 8)
                        for v in range(4):
                            value = jnp.where(keep_row, before[v], after[v])
                            out_ref[2 * s + plane, place, 128 * v : 128 * v + 128] = value
                    before = after
            return inner

        lax.fori_loop(0, groups, block, 0)
        return carry

    lax.fori_loop(0, SOURCES, source_step, 0)
    copy.wait()


def window_call(shifts, pupil, dose):
    vmem = pl.BlockSpec(memory_space=pltpu.VMEM)
    anywhere = pl.BlockSpec(memory_space=pl.ANY)
    return pl.pallas_call(
        window_kernel,
        out_shape=(
            jax.ShapeDtypeStruct((2 * SOURCES, PASS, PASS), jnp.float32),
            jax.ShapeDtypeStruct(dose.shape, jnp.float32),
        ),
        in_specs=[pl.BlockSpec(memory_space=pltpu.SMEM), vmem, anywhere],
        out_specs=(vmem, anywhere),
        scratch_shapes=[pltpu.SemaphoreType.DMA],
        compiler_params=pltpu.CompilerParams(vmem_limit_bytes=20 * MIB),
        cost_estimate=pl.CostEstimate(flops=10_000_000, bytes_accessed=11_000_000, transcendentals=0),
        name="window",
    )(shifts, pupil, dose)


def resist_kernel(
    where_ref, weights_ref, quencher_ref, own_ref, other_ref, window_ref, rows_hbm, cols_hbm,
    dose_ref, side_ref, above_ref, below_ref, acid_ref, inhibitor_ref,
    rows_ref, cols_ref, filt_ref, field_ref, a_ref, b_ref, p_ref, q_ref, sum_ref, sems,
):
    core = where_ref[0]
    rows_copy = pltpu.make_async_copy(rows_hbm.at[where_ref[1]], rows_ref, sems.at[0])
    cols_copy = pltpu.make_async_copy(cols_hbm.at[where_ref[2]], cols_ref, sems.at[1])
    rows_copy.start()
    cols_copy.start()

    def filter_half(s, spec_ref, half, slot):
        def block(o, inner):
            base = pl.multiple_of(o * WIDE, WIDE)
            place = pl.multiple_of(o * FREQS, FREQS)
            row = pl.multiple_of(half * (PASS // 2) + o * FREQS, FREQS)
            real = spec_ref[pl.ds(base, FREQS), :]
            imag = spec_ref[pl.ds(base + FREQS, FREQS), :]
            w_real = window_ref[2 * s, pl.ds(row, FREQS), :]
            w_imag = window_ref[2 * s + 1, pl.ds(row, FREQS), :]
            filt_ref[slot, pl.ds(place, FREQS), :PASS] = (w_real * real - w_imag * imag).astype(jnp.bfloat16)
            filt_ref[slot, pl.ds(place, FREQS), PASS:] = (w_real * imag + w_imag * real).astype(jnp.bfloat16)
            return inner

        lax.fori_loop(0, 16, block, 0, unroll=FILTER_UNROLL)

    def rowfield_half(s, half, slot):
        rowfield = lax.dot_general(
            rows_ref[...], filt_ref[slot], (((1,), (1,)), ((), ())), preferred_element_type=jnp.float32
        ).astype(jnp.bfloat16)
        top = pl.multiple_of(s * TALL, 16)
        left = pl.multiple_of(half * (PASS // 2), PASS // 2)
        field_ref[pl.ds(top, TALL), pl.ds(left, PASS // 2)] = rowfield[:TALL]
        field_ref[pl.ds(top, TALL), pl.ds(PASS + left, PASS // 2)] = rowfield[TALL:]

    def source_step(s, carry):
        filter_half(s, own_ref, core, 0)
        rowfield_half(s, core, 0)
        filter_half(s, other_ref, 1 - core, 1)
        rowfield_half(s, 1 - core, 1)
        return carry

    rows_copy.wait()
    for s in range(SOURCES):
        source_step(s, 0)
    cols_copy.wait()

    row_of = lax.broadcasted_iota(jnp.int32, (8, 128), 0)

    def tile_step(b, carry):
        field = jnp.dot(field_ref[...], cols_ref[b], preferred_element_type=jnp.float32)
        intensity = jnp.zeros((EXT_ROWS, 128), jnp.float32)
        for s in range(SOURCES):
            part = field[s * TALL : s * TALL + EXT_ROWS]
            real, imag = part[:, :128], part[:, 128:]
            intensity = intensity + weights_ref[s] * (real * real + imag * imag)
        lanes = pl.ds(pl.multiple_of(b * 128, 128), 128)
        for z in range(Z):
            bottom = jnp.where(row_of < HALO, below_ref[z, :, lanes], above_ref[z, :, lanes])
            a_ref[z, BRICK_ROWS:, lanes] = 1.0 - jnp.exp(-bottom * intensity[BRICK_ROWS:])

        @pl.when(b < COL_TILES - 1)
        def _():
            for z in range(Z):
                a_ref[z, :BRICK_ROWS, lanes] = 1.0 - jnp.exp(-dose_ref[z, :, lanes] * intensity[:BRICK_ROWS])

        @pl.when(b == COL_TILES - 1)
        def _():
            for z in range(Z):
                a_ref[z, :BRICK_ROWS, lanes] = 1.0 - jnp.exp(-side_ref[z] * intensity[:BRICK_ROWS])

        return carry

    lax.fori_loop(0, COL_TILES, tile_step, 0, unroll=FIELD_UNROLL)

    tiles = EXT_ROWS // 8
    row_id = lax.broadcasted_iota(jnp.int32, (8, EXT_COLS), 0)
    quench = [quencher_ref[0], quencher_ref[1]]

    def neighbours(ref, z, t):
        here = ref[z, pl.ds(pl.multiple_of(t * 8, 8), 8), :]
        before = ref[z, pl.ds(pl.multiple_of(jnp.where(t == 0, tiles - 1, t - 1) * 8, 8), 8), :]
        after = ref[z, pl.ds(pl.multiple_of(jnp.where(t == tiles - 1, 0, t + 1) * 8, 8), 8), :]
        above = pltpu.roll(jnp.where(row_id == 7, before, here), 1, 0)
        below = pltpu.roll(jnp.where(row_id == 0, after, here), 7, 0)
        left = pltpu.roll(here, 1, 1)
        right = pltpu.roll(here, EXT_COLS - 1, 1)
        return here, (above + below) + (left + right)

    buffers = [(a_ref, b_ref), (b_ref, a_ref), (a_ref, b_ref), (b_ref, None)]
    quenches = [(None, p_ref), (p_ref, q_ref), (q_ref, p_ref), (p_ref, None)]
    for step in range(BAKE):
        old, new = buffers[step]
        q_old, q_new = quenches[step]

        def row_step(t, carry):
            rows = pl.ds(pl.multiple_of(t * 8, 8), 8)
            acid = [neighbours(old, z, t) for z in range(Z)]
            acid_z = acid[0][0] + acid[1][0]
            if q_old is None:
                quench_here = quench
                quench_sum = [4.0 * quench[z] for z in range(Z)]
            elif q_new is None:
                quench_here = [q_old[z, rows, :] for z in range(Z)]
            else:
                pairs = [neighbours(q_old, z, t) for z in range(Z)]
                quench_here = [pair[0] for pair in pairs]
                quench_sum = [pair[1] for pair in pairs]
            quench_z = quench_here[0] + quench_here[1]
            for z in range(Z):
                here, around = acid[z]
                reaction = QUENCH_RATE * here * quench_here[z]
                lap = (around + acid_z) - 6.0 * here
                fresh = here + DIFF_ACID * lap - reaction
                if new is not None:
                    new[z, rows, :] = fresh
                else:
                    acid_ref[z, rows, :] = fresh[:, :BRICK_COLS]
                if q_new is not None:
                    q_lap = (quench_sum[z] + quench_z) - 6.0 * quench_here[z]
                    q_new[z, rows, :] = quench_here[z] + DIFF_QUENCH * q_lap - reaction
                if step == 0:
                    sum_ref[z, rows, :] = here[:, :BRICK_COLS]
                elif new is not None:
                    sum_ref[z, rows, :] = sum_ref[z, rows, :] + here[:, :BRICK_COLS]
                else:
                    total = sum_ref[z, rows, :] + here[:, :BRICK_COLS]
                    inhibitor_ref[z, rows, :] = jnp.exp(-CATALYSIS * total)
            return carry

        lax.fori_loop(0, tiles if new is not None else BRICK_ROWS // 8, row_step, 0, unroll=BAKE_UNROLL)


def resist_call(where, weights, quencher, own, other, window, rows, cols, dose, side, above, below):
    smem = pl.BlockSpec(memory_space=pltpu.SMEM)
    vmem = pl.BlockSpec(memory_space=pltpu.VMEM)
    hbm = pl.BlockSpec(memory_space=pl.ANY)
    out = jax.ShapeDtypeStruct((Z, BRICK_ROWS, BRICK_COLS), jnp.float32)
    brick = pltpu.VMEM((Z, EXT_ROWS, EXT_COLS), jnp.float32)
    return pl.pallas_call(
        resist_kernel,
        out_shape=(out, out),
        in_specs=[smem] * 3 + [vmem] * 3 + [hbm] * 2 + [vmem] * 4,
        out_specs=(vmem, vmem),
        scratch_shapes=[
            pltpu.VMEM(rows.shape[1:], jnp.bfloat16),
            pltpu.VMEM(cols.shape[1:], jnp.bfloat16),
            pltpu.VMEM((2, PASS // 2, 2 * PASS), jnp.bfloat16),
            pltpu.VMEM((SOURCES * TALL, 2 * PASS), jnp.bfloat16),
            brick, brick, brick, brick,
            pltpu.VMEM((Z, EXT_ROWS, BRICK_COLS), jnp.float32),
            pltpu.SemaphoreType.DMA((2,)),
        ],
        compiler_params=pltpu.CompilerParams(vmem_limit_bytes=28 * MIB),
        name="resist",
    )(where, weights, quencher, own, other, window, rows, cols, dose, side, above, below)


def ring(axes, step):
    size = lax.axis_size(axes)
    return [(i, (i + step) % size) for i in range(size)]


def body(mask_ids, trans_table, pupil, shifts, weights, dose, quencher):
    src_axes, tile_axes = ("zl", "c"), ("y", "zh", "x")
    core, src, tile = lax.axis_index("c"), lax.axis_index(src_axes), lax.axis_index(tile_axes)
    packed = columns_call(trans_table, mask_ids, jnp.asarray(forward_columns()), jnp.asarray(edge_columns()))
    packed, shifts, weights, dose_late, pupil = lax.optimization_barrier((packed, shifts, weights, dose, pupil))
    cols = lax.all_to_all(packed, ALL, 0, 0, tiled=True)

    turned, last, first, note = pack_call(shifts, weights, pupil, dose_late)
    before = lax.ppermute(last, src_axes, ring(src_axes, 1))
    after = lax.ppermute(first, src_axes, ring(src_axes, -1))
    far = lax.ppermute(note, src_axes, ring(src_axes, 2))
    notes = [note[:1, 64:67], far[:1, 64:67], before[0, :1, 64:67], after[0, :1, 64:67]]
    sources = jnp.concatenate(notes, axis=0)
    all_shifts, all_weights = sources[:, :2].astype(jnp.int32), sources[:, 2]
    side, last, first = edge_call(dose_late, before, after)
    above = lax.ppermute(last, tile_axes, ring(tile_axes, 1))
    below = lax.ppermute(first, tile_axes, ring(tile_axes, -1))
    where = jnp.stack([core, tile, src]).astype(jnp.int32)

    block = spectrum_call(jnp.asarray(forward_rows()), cols, jnp.asarray(edge_rows()))
    own = lax.all_to_all(block, ("y", "x"), 0, 0, tiled=True)
    own, turned, all_shifts, all_weights, side, above, below, where = lax.optimization_barrier(
        (own, turned, all_shifts, all_weights, side, above, below, where)
    )
    other = lax.ppermute(own, "c", [(0, 1), (1, 0)])
    window, dose_near = window_call(all_shifts, turned, dose)
    return resist_call(
        where, all_weights, quencher, own, other, window,
        jnp.asarray(inverse_rows(32)), jnp.asarray(inverse_cols(4)), dose_near, side, above, below,
    )


def solution(mesh):
    parts = Mesh(mesh.devices.reshape(2, 2, 4, 2, 4), ALL)
    src, tile = ("zl", "c"), ("y", "zh", "x")
    inner = jax.shard_map(
        body,
        mesh=parts,
        in_specs=(
            P(ALL, None),
            P(),
            P(),
            P(src, None),
            P(src),
            P(None, tile, src),
            P(),
        ),
        out_specs=(P(None, tile, src), P(None, tile, src)),
        check_vma=False,
    )
    return inner
```

```python
import math

import jax
import jax.numpy as jnp
import numpy as np
from jax import lax
from jax.experimental import pallas as pl
from jax.experimental.pallas import tpu as pltpu
from jax.sharding import Mesh, PartitionSpec as P

NPIX = 4096
PASS = 512
SHIFT = 64
LEVELS = 4
SOURCES = 4
BAKE = 4
Z = 2
PUPIL_TILES = (PASS + 2 * SHIFT) // 8
DIFF_ACID = 0.12
DIFF_QUENCH = 0.04
QUENCH_RATE = 0.6
CATALYSIS = 0.4

DEVICES = 128
ROWS = NPIX // DEVICES
OWNERS = 32
FREQS = PASS // OWNERS
WIDE = 2 * FREQS
HALO = 4
TALL = 144
BRICK_ROWS = 128
BRICK_COLS = 1024
EXT_ROWS = BRICK_ROWS + 2 * HALO
EXT_COLS = BRICK_COLS + 128
COL_TILES = EXT_COLS // 128
EARLY = 2
ALL = ("zl", "c", "y", "zh", "x")
MIB = 1024 * 1024


def cos_sin(first, second):
    theta = (np.mod(first[:, None] * second[None, :], NPIX)).astype(np.float32)
    theta = (theta * np.float32(2.0 * math.pi / NPIX)).astype(np.float64)
    return np.cos(theta).astype(np.float32), np.sin(theta).astype(np.float32)


def bf16(table):
    return table.astype(jnp.bfloat16)


FREQ = np.arange(PASS, dtype=np.int64) - PASS // 2
HALF = PASS // 2


def forward_columns():
    return bf16(np.concatenate(cos_sin(np.arange(NPIX), np.arange(HALF)), axis=1))


def forward_rows():
    order = np.arange(NPIX).reshape(DEVICES, 4, 8).transpose(1, 0, 2).reshape(NPIX)
    both = np.concatenate(cos_sin(np.arange(HALF), order), axis=0)
    return bf16(both.reshape(PASS, 4, NPIX // 4).transpose(1, 0, 2))


def edge_columns():
    cosine, sine = cos_sin(np.array([HALF]), np.arange(128))
    return np.asarray(bf16(np.concatenate([cosine, sine], axis=0))).astype(np.float32)


def edge_rows():
    rows = np.arange(4)[None, :] * 8 + np.arange(8)[:, None]
    cosine, sine = cos_sin(np.array([HALF]), rows.reshape(-1))
    both = np.stack([cosine.reshape(8, 4), sine.reshape(8, 4)])
    return np.asarray(bf16(np.repeat(both, WIDE, axis=2))).astype(np.float32)


def inverse_rows(tiles):
    blocks = []
    for tile in range(tiles):
        local = np.arange(TALL)
        local = np.where(local < BRICK_ROWS + HALO, local, local - EXT_ROWS)
        pixels = np.mod(tile * BRICK_ROWS + local, NPIX)
        cosine, sine = cos_sin(pixels, FREQ)
        upper = np.concatenate([cosine, -sine], axis=1)
        lower = np.concatenate([sine, cosine], axis=1)
        blocks.append(np.concatenate([upper, lower], axis=0))
    return bf16(np.stack(blocks))


def inverse_cols(sources):
    lanes = np.arange(EXT_COLS)
    local = np.where(lanes < BRICK_COLS + 64, lanes, lanes - EXT_COLS)
    blocks = []
    for source in range(sources):
        pixels = np.mod(source * BRICK_COLS + local, NPIX)
        cosine, sine = cos_sin(FREQ, pixels)
        real = np.concatenate([cosine, -sine], axis=0).reshape(2 * PASS, COL_TILES, 1, 128)
        imag = np.concatenate([sine, cosine], axis=0).reshape(2 * PASS, COL_TILES, 1, 128)
        both = np.concatenate([real, imag], axis=2).reshape(2 * PASS, COL_TILES, 256)
        blocks.append(both.transpose(1, 0, 2))
    return bf16(np.stack(blocks))


def lane_ids(shape):
    return lax.broadcasted_iota(jnp.int32, shape, len(shape) - 1)


def columns_kernel(trans_ref, ids_ref, table_ref, edge_ref, out_ref, acc_ref, sum_ref, perm_ref):
    step = pl.program_id(0)

    @pl.when(step == 0)
    def _():
        acc_ref[...] = jnp.zeros_like(acc_ref)
        sum_ref[...] = jnp.zeros_like(sum_ref)
        source = lax.broadcasted_iota(jnp.int32, (PASS, PASS), 0)
        lane = lax.broadcasted_iota(jnp.int32, (PASS, PASS), 1)
        plane, place = lane // FREQS % 2, lane // WIDE * FREQS + lane % FREQS
        perm_ref[0] = (source == plane * HALF + (HALF - place) % HALF).astype(jnp.float32).astype(jnp.bfloat16)
        perm_ref[1] = (source == plane * HALF + place).astype(jnp.float32).astype(jnp.bfloat16)

    ids = ids_ref[...]
    parts = []
    for plane in range(2):
        value = jnp.zeros(ids.shape, jnp.float32)
        for level in range(LEVELS):
            value = jnp.where(ids == level, trans_ref[plane, level], value)
        parts.append(value)
    trans = jnp.concatenate(parts, axis=0).astype(jnp.bfloat16)
    acc_ref[...] += jnp.dot(trans, table_ref[...], preferred_element_type=jnp.float32)
    exact = trans.astype(jnp.float32)
    total = sum_ref[...]
    for tile in range(ids.shape[1] // 128):
        total = total + exact[:, 128 * tile : 128 * tile + 128]
    sum_ref[...] = total

    @pl.when(step == pl.num_programs(0) - 1)
    def _():
        edge_cos = jnp.sum(sum_ref[...] * edge_ref[0:1, :], axis=1, keepdims=True)
        edge_sin = jnp.sum(sum_ref[...] * edge_ref[1:2, :], axis=1, keepdims=True)
        cos_real, cos_imag = acc_ref[:ROWS, :HALF], acc_ref[ROWS:, :HALF]
        sin_real, sin_imag = acc_ref[:ROWS, HALF:], acc_ref[ROWS:, HALF:]
        first = lane_ids((ROWS, HALF)) == 0
        low_real = jnp.where(first, edge_cos[:ROWS] - edge_sin[ROWS:], cos_real - sin_imag)
        low_imag = jnp.where(first, edge_cos[ROWS:] + edge_sin[:ROWS], cos_imag + sin_real)
        low = jnp.concatenate([low_real, low_imag], axis=1).astype(jnp.bfloat16)
        high = jnp.concatenate([cos_real + sin_imag, cos_imag - sin_real], axis=1).astype(jnp.bfloat16)
        sides = [
            jnp.dot(low, perm_ref[0], preferred_element_type=jnp.float32),
            jnp.dot(high, perm_ref[1], preferred_element_type=jnp.float32),
        ]
        group = lane_ids((8, 128)) // WIDE
        chunks = []
        for owner in range(OWNERS):
            major, minor = owner % 16 // 4, owner % 4
            chunk = jnp.zeros((8, 128), jnp.float32)
            for q in range(4):
                piece = sides[owner // 16][8 * q : 8 * q + 8, 128 * major : 128 * major + 128]
                turn = (q - minor) % 4 * WIDE
                piece = pltpu.roll(piece, turn, 1) if turn else piece
                chunk = jnp.where(group == q, piece, chunk)
            chunks.append(chunk)
        for pair in range(DEVICES // 2):
            both = []
            for dest in (2 * pair, 2 * pair + 1):
                core, y, x = dest // 32 % 2, dest // 8 % 4, dest % 4
                both.append(chunks[core * 16 + y * 4 + x])
            out_ref[16 * pair : 16 * pair + 16, :] = jnp.concatenate(both, axis=0).astype(jnp.bfloat16)


def columns_call(trans_table, mask_ids, table, edge):
    steps = 4
    depth = NPIX // steps
    return pl.pallas_call(
        columns_kernel,
        grid=(steps,),
        out_shape=jax.ShapeDtypeStruct((DEVICES * 8, 128), jnp.bfloat16),
        in_specs=[
            pl.BlockSpec(memory_space=pltpu.SMEM),
            pl.BlockSpec((ROWS, depth), lambda k: (0, k)),
            pl.BlockSpec((depth, PASS), lambda k: (k, 0)),
            pl.BlockSpec((2, 128), lambda k: (0, 0)),
        ],
        out_specs=pl.BlockSpec((DEVICES * 8, 128), lambda k: (0, 0)),
        scratch_shapes=[
            pltpu.VMEM((2 * ROWS, PASS), jnp.float32),
            pltpu.VMEM((2 * ROWS, 128), jnp.float32),
            pltpu.VMEM((2, PASS, PASS), jnp.bfloat16),
        ],
        compiler_params=pltpu.CompilerParams(vmem_limit_bytes=56 * MIB),
        name="columns",
    )(trans_table, mask_ids, table, edge)


def spectrum_kernel(table_ref, cols_ref, edge_ref, out_ref, acc_ref):
    step = pl.program_id(0)
    product = jnp.dot(table_ref[0], cols_ref[...], preferred_element_type=jnp.float32)
    group = lane_ids(product.shape) // WIDE

    @pl.when(step == 0)
    def _():
        acc_ref[...] = product

    @pl.when(step > 0)
    def _():
        acc_ref[...] = jnp.where(group == step, product, acc_ref[...])

    @pl.when(step == pl.num_programs(0) - 1)
    def _():
        columns = cols_ref[...].astype(jnp.float32)
        total = [columns[16 * k : 16 * k + 16] for k in range(DEVICES // 2)]
        while len(total) > 1:
            total = [a + b for a, b in zip(total[::2], total[1::2])]
        total = total[0][:8] + total[0][8:]
        edge_cos = jnp.sum(total * edge_ref[0], axis=0, keepdims=True)
        edge_sin = jnp.sum(total * edge_ref[1], axis=0, keepdims=True)

        def fold(value):
            value = value + pltpu.roll(value, 64, 1)
            return value + pltpu.roll(value, 32, 1)

        def turn(value):
            is_real = lane_ids(value.shape) % WIDE < FREQS
            return jnp.where(is_real, pltpu.roll(value, 128 - FREQS, 1), -pltpu.roll(value, FREQS, 1))

        edges = fold(jnp.concatenate([edge_cos, edge_sin, jnp.zeros((6, 128), jnp.float32)], axis=0))
        edge = edges[0:1] - turn(edges)[1:2]
        folded = fold(acc_ref[...])
        cosine, turned = folded[:HALF], turn(folded[HALF:])
        first = lax.broadcasted_iota(jnp.int32, cosine.shape, 0) == 0
        scale = 1.0 / (NPIX * NPIX)
        high = jnp.transpose((cosine + turned) * scale)[:WIDE]
        low = jnp.transpose(jnp.where(first, edge, cosine - turned) * scale)[:WIDE]
        source = lax.broadcasted_iota(jnp.int32, (HALF, HALF), 0)
        place = lax.broadcasted_iota(jnp.int32, (HALF, HALF), 1)
        perm = (source == (HALF - place) % HALF).astype(jnp.float32).astype(jnp.bfloat16)
        pieces = []
        rest = low
        for _ in range(3):
            piece = rest.astype(jnp.bfloat16)
            rest = rest - piece.astype(jnp.float32)
            pieces.append(jnp.dot(piece, perm, preferred_element_type=jnp.float32))
        block = jnp.concatenate([pieces[0] + pieces[1] + pieces[2], high], axis=1)
        for dest in range(16):
            out_ref[dest * WIDE : (dest + 1) * WIDE, :] = block


def spectrum_call(table, cols, edge):
    return pl.pallas_call(
        spectrum_kernel,
        grid=(4,),
        out_shape=jax.ShapeDtypeStruct((16 * WIDE, PASS), jnp.float32),
        in_specs=[
            pl.BlockSpec((1, PASS, NPIX // 4), lambda q: (q, 0, 0)),
            pl.BlockSpec((NPIX // 4, 128), lambda q: (0, 0)),
            pl.BlockSpec((2, 8, 128), lambda q: (0, 0, 0)),
        ],
        out_specs=pl.BlockSpec((16 * WIDE, PASS), lambda q: (0, 0)),
        scratch_shapes=[pltpu.VMEM((PASS, 128), jnp.float32)],
        compiler_params=pltpu.CompilerParams(vmem_limit_bytes=16 * MIB),
        name="spectrum",
    )(table, cols, edge)


def pack_kernel(shifts_ref, weights_ref, pupil_ref, dose_ref, turned_ref, last_ref, first_ref, note_ref):
    blocks = pupil_ref.shape[1] // 128
    for plane in range(2):
        for i in range(blocks):
            for j in range(blocks):
                piece = pupil_ref[plane, 128 * i : 128 * i + 128, 128 * j : 128 * j + 128]
                turned_ref[plane, 128 * j : 128 * j + 128, 128 * i : 128 * i + 128] = jnp.transpose(piece)

    def note(shape):
        lane = lane_ids(shape)
        shift_x, shift_y = shifts_ref[0, 0].astype(jnp.float32), shifts_ref[0, 1].astype(jnp.float32)
        return jnp.where(lane == 64, shift_x, jnp.where(lane == 65, shift_y, weights_ref[0]))

    lane = lane_ids((BRICK_ROWS, 128))
    middle = (lane >= 64) & (lane < 67)
    for z in range(Z):
        last_ref[z] = jnp.where(middle, note((BRICK_ROWS, 128)), dose_ref[z, :, BRICK_COLS - 128 :])
        first_ref[z] = jnp.where(middle, note((BRICK_ROWS, 128)), dose_ref[z, :, :128])
    note_ref[...] = note((8, 128))


def pack_call(shifts, weights, pupil, dose):
    vmem = pl.BlockSpec(memory_space=pltpu.VMEM)
    smem = pl.BlockSpec(memory_space=pltpu.SMEM)
    side = jax.ShapeDtypeStruct((Z, BRICK_ROWS, 128), jnp.float32)
    return pl.pallas_call(
        pack_kernel,
        out_shape=(
            jax.ShapeDtypeStruct(pupil.shape, jnp.float32),
            side,
            side,
            jax.ShapeDtypeStruct((8, 128), jnp.float32),
        ),
        in_specs=[smem, smem, vmem, vmem],
        out_specs=(vmem,) * 4,
        compiler_params=pltpu.CompilerParams(vmem_limit_bytes=12 * MIB),
        cost_estimate=pl.CostEstimate(flops=1_000_000, bytes_accessed=9_000_000, transcendentals=0),
        name="pack",
    )(shifts, weights, pupil, dose)


def edge_kernel(dose_ref, before_ref, after_ref, side_ref, last_ref, first_ref):
    lane = lane_ids((BRICK_ROWS, 128))
    for z in range(Z):
        side = jnp.where(lane < 64, after_ref[z], before_ref[z])
        side_ref[z] = side
        last_ref[z, :, :BRICK_COLS] = dose_ref[z, BRICK_ROWS - 8 :, :]
        last_ref[z, :, BRICK_COLS:] = side[BRICK_ROWS - 8 :]
        first_ref[z, :, :BRICK_COLS] = dose_ref[z, :8, :]
        first_ref[z, :, BRICK_COLS:] = side[:8]


def edge_call(dose, before, after):
    vmem = pl.BlockSpec(memory_space=pltpu.VMEM)
    row = jax.ShapeDtypeStruct((Z, 8, EXT_COLS), jnp.float32)
    return pl.pallas_call(
        edge_kernel,
        out_shape=(jax.ShapeDtypeStruct((Z, BRICK_ROWS, 128), jnp.float32), row, row),
        in_specs=[vmem] * 3,
        out_specs=(vmem,) * 3,
        compiler_params=pltpu.CompilerParams(vmem_limit_bytes=6 * MIB),
        cost_estimate=pl.CostEstimate(flops=1_000_000, bytes_accessed=2_000_000, transcendentals=0),
        name="edge",
    )(dose, before, after)


def window_kernel(shifts_ref, turned_ref, out_hbm, token_ref, out_ref, sems):
    token_ref[...] = jnp.zeros_like(token_ref)
    lane = lane_ids((8, 128))
    row = lax.broadcasted_iota(jnp.int32, (8, 128), 0)
    zero = jnp.zeros((8, 128), jnp.float32)
    tiles, group, groups = PASS // 8, 13, 4
    edge = SHIFT * 2 // 8

    def source_step(s, carry):
        lift = SHIFT - shifts_ref[s, 1]
        shift = SHIFT - shifts_ref[s, 0]
        first, rest = lift // 8, lax.rem(lift, 8)
        rise = lax.rem(8 - rest, 8)
        turn = lax.rem(256 - shift, 128)
        keep_lane = lane < 128 - shift
        keep_row = row < 8 - rest
        begin = jnp.minimum(edge - first - jnp.where(rest > 0, 1, 0), tiles - group * groups)

        def clear(t, inner):
            for plane in range(2):
                for v in range(4):
                    out_ref[2 * s + plane, pl.ds(pl.multiple_of(t * 8, 8), 8), 128 * v : 128 * v + 128] = zero
            return inner

        lax.fori_loop(0, begin, clear, 0)
        lax.fori_loop(begin + group * groups, tiles, clear, 0)

        def block(t, inner):
            start = begin + t * group
            for plane in range(2):
                before = None
                for k in range(group + 1):
                    tile = jnp.minimum(start + k + first, PUPIL_TILES - 1)
                    base = pl.ds(pl.multiple_of(tile * 8, 8), 8)
                    turned = [zero] + [
                        pltpu.roll(turned_ref[plane, base, 128 * v : 128 * v + 128], turn, 1) for v in range(1, 5)
                    ]
                    cut = [jnp.where(keep_lane, turned[v], turned[v + 1]) for v in range(4)]
                    after = [pltpu.roll(c, rise, 0) for c in cut]
                    if before is not None:
                        place = pl.ds(pl.multiple_of((start + k - 1) * 8, 8), 8)
                        for v in range(4):
                            value = jnp.where(keep_row, before[v], after[v])
                            out_ref[2 * s + plane, place, 128 * v : 128 * v + 128] = value
                    before = after
            return inner

        lax.fori_loop(0, groups, block, 0)
        leave(s).start()
        return carry

    def leave(s):
        planes = pl.ds(2 * s, 2)
        return pltpu.make_async_copy(out_ref.at[planes], out_hbm.at[planes], sems.at[s])

    lax.fori_loop(0, SOURCES, source_step, 0)
    for s in range(SOURCES):
        leave(s).wait()


def window_call(shifts, pupil):
    vmem = pl.BlockSpec(memory_space=pltpu.VMEM)
    planes = 2 * SOURCES
    return pl.pallas_call(
        window_kernel,
        out_shape=(
            jax.ShapeDtypeStruct((3 * planes, PASS, PASS), jnp.float32),
            jax.ShapeDtypeStruct((8, 128), jnp.float32),
        ),
        in_specs=[pl.BlockSpec(memory_space=pltpu.SMEM), vmem],
        out_specs=(pl.BlockSpec(memory_space=pl.ANY), vmem),
        scratch_shapes=[pltpu.VMEM((planes, PASS, PASS), jnp.float32), pltpu.SemaphoreType.DMA((SOURCES,))],
        compiler_params=pltpu.CompilerParams(vmem_limit_bytes=44 * MIB),
        cost_estimate=pl.CostEstimate(flops=10_000_000, bytes_accessed=11_000_000, transcendentals=0),
        name="window",
    )(shifts, pupil)


def rowfield_half(s, spec_ref, window_ref, rows_ref, filt_ref):
    slot = s % 2

    def block(o, inner):
        base = pl.multiple_of(o * WIDE, WIDE)
        place = pl.ds(pl.multiple_of(o * FREQS, FREQS), FREQS)
        real = spec_ref[pl.ds(base, FREQS), :]
        imag = spec_ref[pl.ds(base + FREQS, FREQS), :]
        w_real = window_ref[2 * s, place, :]
        w_imag = window_ref[2 * s + 1, place, :]
        filt_ref[slot, place, :PASS] = (w_real * real - w_imag * imag).astype(jnp.bfloat16)
        filt_ref[slot, place, PASS:] = (w_real * imag + w_imag * real).astype(jnp.bfloat16)
        return inner

    lax.fori_loop(0, 16, block, 0, unroll=16)
    return lax.dot_general(
        rows_ref[...], filt_ref[slot], (((1,), (1,)), ((), ())), preferred_element_type=jnp.float32
    ).astype(jnp.bfloat16)


def own_kernel(
    where_ref, token_ref, own_ref, window_hbm, rows_hbm, dose_hbm,
    field_ref, rows_ref, other_ref, dose_ref, window_ref, filt_ref, sems,
):
    core = where_ref[0]
    mine = pl.ds(pl.multiple_of(core * HALF, HALF), HALF)
    theirs = pl.ds(pl.multiple_of((1 - core) * HALF, HALF), HALF)
    rows_copy = pltpu.make_async_copy(rows_hbm.at[where_ref[1]], rows_ref, sems.at[0])
    rows_copy.start()
    copies = []
    for s in range(SOURCES):
        planes = pl.ds(2 * s, 2)
        copies.append(pltpu.make_async_copy(window_hbm.at[planes, mine], window_ref.at[planes], sems.at[1 + s]))
        copies[s].start()
    later = [
        pltpu.make_async_copy(dose_hbm, dose_ref, sems.at[1 + SOURCES]),
        pltpu.make_async_copy(window_hbm.at[pl.ds(0, 2 * SOURCES), theirs], other_ref, sems.at[2 + SOURCES]),
    ]
    for copy in later:
        copy.start()
    rows_copy.wait()
    for s in range(SOURCES):
        if s % 2 == 0:
            copies[s].wait()
            copies[s + 1].wait()
        rowfield = rowfield_half(s, own_ref, window_ref, rows_ref, filt_ref)
        field_ref[s * TALL : (s + 1) * TALL, :HALF] = rowfield[:TALL]
        field_ref[s * TALL : (s + 1) * TALL, HALF:] = rowfield[TALL:]
    for copy in later:
        copy.wait()


def own_call(where, token, own, window, rows, dose):
    smem = pl.BlockSpec(memory_space=pltpu.SMEM)
    vmem = pl.BlockSpec(memory_space=pltpu.VMEM)
    hbm = pl.BlockSpec(memory_space=pl.ANY)
    half = (2 * SOURCES, HALF, PASS)
    return pl.pallas_call(
        own_kernel,
        out_shape=(
            jax.ShapeDtypeStruct((SOURCES * TALL, PASS), jnp.bfloat16),
            jax.ShapeDtypeStruct(rows.shape[1:], jnp.bfloat16),
            jax.ShapeDtypeStruct(half, jnp.float32),
            jax.ShapeDtypeStruct(dose.shape, jnp.float32),
        ),
        in_specs=[smem, hbm, vmem, hbm, hbm, hbm],
        out_specs=(vmem,) * 4,
        scratch_shapes=[
            pltpu.VMEM(half, jnp.float32),
            pltpu.VMEM((2, HALF, 2 * PASS), jnp.bfloat16),
            pltpu.SemaphoreType.DMA((3 + SOURCES,)),
        ],
        compiler_params=pltpu.CompilerParams(vmem_limit_bytes=36 * MIB),
        cost_estimate=pl.CostEstimate(flops=10_000_000, bytes_accessed=9_000_000, transcendentals=0),
        name="own_half",
    )(where, token, own, window, rows, dose)


def resist_kernel(
    where_ref, weights_ref, quencher_ref, half_ref, other_ref, window_ref, rows_ref, cols_hbm,
    dose_ref, side_ref, above_ref, below_ref, acid_hbm, inhibitor_hbm,
    cols_ref, filt_ref, field_ref, a_ref, b_ref, p_ref, q_ref, sum_ref, acid_ref, inhibitor_ref, sems, out_sems,
):
    core = where_ref[0]
    cols_copies = []
    for k, (begin, count) in enumerate(((0, EARLY), (EARLY, COL_TILES - EARLY))):
        part = pl.ds(begin, count)
        cols_copies.append(pltpu.make_async_copy(cols_hbm.at[where_ref[2], part], cols_ref.at[part], sems.at[k]))
        cols_copies[k].start()
    mine = pl.multiple_of(core * HALF, HALF)
    theirs = pl.multiple_of((1 - core) * HALF, HALF)
    field_ref[:, pl.ds(mine, HALF)] = half_ref[:, :HALF]
    field_ref[:, pl.ds(PASS + mine, HALF)] = half_ref[:, HALF:]
    for s in range(SOURCES):
        rowfield = rowfield_half(s, other_ref, window_ref, rows_ref, filt_ref)
        field_ref[s * TALL : (s + 1) * TALL, pl.ds(theirs, HALF)] = rowfield[:TALL]
        field_ref[s * TALL : (s + 1) * TALL, pl.ds(PASS + theirs, HALF)] = rowfield[TALL:]
    cols_copies[0].wait()
    row_of = lax.broadcasted_iota(jnp.int32, (8, 128), 0)

    for b in range(COL_TILES):
        if b == EARLY:
            cols_copies[1].wait()
        field = jnp.dot(field_ref[...], cols_ref[b], preferred_element_type=jnp.float32)
        intensity = jnp.zeros((EXT_ROWS, 128), jnp.float32)
        for s in range(SOURCES):
            part = field[s * TALL : s * TALL + EXT_ROWS]
            real, imag = part[:, :128], part[:, 128:]
            intensity = intensity + weights_ref[s] * (real * real + imag * imag)
        lanes = slice(b * 128, b * 128 + 128)
        for z in range(Z):
            bottom = jnp.where(row_of < HALO, below_ref[z, :, lanes], above_ref[z, :, lanes])
            middle = dose_ref[z, :, lanes] if b < COL_TILES - 1 else side_ref[z]
            a_ref[z, :BRICK_ROWS, lanes] = QUENCH_RATE - QUENCH_RATE * jnp.exp(-middle * intensity[:BRICK_ROWS])
            a_ref[z, BRICK_ROWS:, lanes] = QUENCH_RATE - QUENCH_RATE * jnp.exp(-bottom * intensity[BRICK_ROWS:])

    tiles = EXT_ROWS // 8
    row_id = lax.broadcasted_iota(jnp.int32, (8, EXT_COLS), 0)
    quench = [QUENCH_RATE * quencher_ref[0], QUENCH_RATE * quencher_ref[1]]

    def neighbours(ref, z, t):
        here = ref[z, 8 * t : 8 * t + 8, :]
        up, down = (t - 1) % tiles, (t + 1) % tiles
        above = pltpu.roll(jnp.where(row_id == 7, ref[z, 8 * up : 8 * up + 8, :], here), 1, 0)
        below = pltpu.roll(jnp.where(row_id == 0, ref[z, 8 * down : 8 * down + 8, :], here), 7, 0)
        left = pltpu.roll(here, 1, 1)
        right = pltpu.roll(here, EXT_COLS - 1, 1)
        return here, (above + below) + (left + right)

    buffers = [(a_ref, b_ref), (b_ref, a_ref), (a_ref, b_ref), (b_ref, None)]
    quenches = [(None, p_ref), (p_ref, q_ref), (q_ref, p_ref), (p_ref, None)]
    copies = []
    for step in range(BAKE):
        old, new = buffers[step]
        q_old, q_new = quenches[step]
        for t in range(tiles if new is not None else BRICK_ROWS // 8):
            rows = slice(8 * t, 8 * t + 8)
            acid = [neighbours(old, z, t) for z in range(Z)]
            acid_z = acid[0][0] + acid[1][0]
            if q_old is None:
                quench_here = quench
                quench_sum = [4.0 * quench[z] for z in range(Z)]
            elif q_new is None:
                quench_here = [q_old[z, rows, :] for z in range(Z)]
            else:
                pairs = [neighbours(q_old, z, t) for z in range(Z)]
                quench_here = [pair[0] for pair in pairs]
                quench_sum = [pair[1] for pair in pairs]
            quench_z = quench_here[0] + quench_here[1]
            for z in range(Z):
                here, around = acid[z]
                reaction = here * quench_here[z]
                fresh = ((1.0 - 6.0 * DIFF_ACID) * here + DIFF_ACID * (around + acid_z)) - reaction
                if new is not None:
                    new[z, rows, :] = fresh
                else:
                    acid_ref[z, rows, :] = fresh[:, :BRICK_COLS] * (1.0 / QUENCH_RATE)
                if q_new is not None:
                    kept = (1.0 - 6.0 * DIFF_QUENCH) * quench_here[z]
                    q_new[z, rows, :] = (kept + DIFF_QUENCH * (quench_sum[z] + quench_z)) - reaction
                if t < BRICK_ROWS // 8:
                    if step == 0:
                        sum_ref[z, rows, :] = here[:, :BRICK_COLS]
                    elif new is not None:
                        sum_ref[z, rows, :] = sum_ref[z, rows, :] + here[:, :BRICK_COLS]
                    else:
                        total = sum_ref[z, rows, :] + here[:, :BRICK_COLS]
                        inhibitor_ref[z, rows, :] = jnp.exp((-CATALYSIS / QUENCH_RATE) * total)
            if new is None and t % 4 == 3:
                ready = pl.ds(8 * (t - 3), 32)
                for k, (near, far) in enumerate(((acid_ref, acid_hbm), (inhibitor_ref, inhibitor_hbm))):
                    copy = pltpu.make_async_copy(near.at[:, ready], far.at[:, ready], out_sems.at[t // 4, k])
                    copy.start()
                    copies.append(copy)
    for copy in copies:
        copy.wait()


def resist_call(where, weights, quencher, half, other, window, rows, cols, dose, side, above, below):
    smem = pl.BlockSpec(memory_space=pltpu.SMEM)
    vmem = pl.BlockSpec(memory_space=pltpu.VMEM)
    hbm = pl.BlockSpec(memory_space=pl.ANY)
    brick_shape = (Z, BRICK_ROWS, BRICK_COLS)
    out = jax.ShapeDtypeStruct(brick_shape, jnp.float32)
    brick = pltpu.VMEM((Z, EXT_ROWS, EXT_COLS), jnp.float32)
    near = pltpu.VMEM(brick_shape, jnp.float32)
    return pl.pallas_call(
        resist_kernel,
        out_shape=(out, out),
        in_specs=[smem] * 3 + [vmem] * 4 + [hbm] + [vmem] * 4,
        out_specs=(hbm, hbm),
        scratch_shapes=[
            pltpu.VMEM(cols.shape[1:], jnp.bfloat16),
            pltpu.VMEM((2, HALF, 2 * PASS), jnp.bfloat16),
            pltpu.VMEM((SOURCES * TALL, 2 * PASS), jnp.bfloat16),
            brick, brick, brick, brick,
            near, near, near,
            pltpu.SemaphoreType.DMA((2,)),
            pltpu.SemaphoreType.DMA((4, 2)),
        ],
        compiler_params=pltpu.CompilerParams(vmem_limit_bytes=46 * MIB),
        name="resist",
    )(where, weights, quencher, half, other, window, rows, cols, dose, side, above, below)


def ring(axes, step):
    size = lax.axis_size(axes)
    return [(i, (i + step) % size) for i in range(size)]


def body(mask_ids, trans_table, pupil, shifts, weights, dose, quencher):
    src_axes, tile_axes = ("zl", "c"), ("y", "zh", "x")
    core, src, tile = lax.axis_index("c"), lax.axis_index(src_axes), lax.axis_index(tile_axes)
    packed = columns_call(trans_table, mask_ids, jnp.asarray(forward_columns()), jnp.asarray(edge_columns()))
    packed, shifts, weights, dose_late, pupil = lax.optimization_barrier((packed, shifts, weights, dose, pupil))
    cols = lax.all_to_all(packed, ALL, 0, 0, tiled=True)

    turned, last, first, note = pack_call(shifts, weights, pupil, dose_late)
    before = lax.ppermute(last, src_axes, ring(src_axes, 1))
    after = lax.ppermute(first, src_axes, ring(src_axes, -1))
    far = lax.ppermute(note, src_axes, ring(src_axes, 2))
    notes = [note[:1, 64:67], far[:1, 64:67], before[0, :1, 64:67], after[0, :1, 64:67]]
    sources = jnp.concatenate(notes, axis=0)
    all_shifts, all_weights = sources[:, :2].astype(jnp.int32), sources[:, 2]
    side, last, first = edge_call(dose_late, before, after)
    above = lax.ppermute(last, tile_axes, ring(tile_axes, 1))
    below = lax.ppermute(first, tile_axes, ring(tile_axes, -1))
    where = jnp.stack([core, tile, src]).astype(jnp.int32)

    block = spectrum_call(jnp.asarray(forward_rows()), cols, jnp.asarray(edge_rows()))
    own = lax.all_to_all(block, ("y", "x"), 0, 0, tiled=True)
    window, token = window_call(all_shifts, turned)
    own, token, all_weights, side, above, below, where = lax.optimization_barrier(
        (own, token, all_weights, side, above, below, where)
    )
    other = lax.ppermute(own, "c", [(0, 1), (1, 0)])
    half, row_table, window_other, dose_near = own_call(where, token, own, window, jnp.asarray(inverse_rows(32)), dose)
    return resist_call(
        where, all_weights, quencher, half, other, window_other, row_table,
        jnp.asarray(inverse_cols(4)), dose_near, side, above, below,
    )


def solution(mesh):
    parts = Mesh(mesh.devices.reshape(2, 2, 4, 2, 4), ALL)
    src, tile = ("zl", "c"), ("y", "zh", "x")
    inner = jax.shard_map(
        body,
        mesh=parts,
        in_specs=(
            P(ALL, None),
            P(),
            P(),
            P(src, None),
            P(src),
            P(None, tile, src),
            P(),
        ),
        out_specs=(P(None, tile, src), P(None, tile, src)),
        check_vma=False,
    )
    return inner
```

```python
import math

import jax
import jax.numpy as jnp
import numpy as np
from jax import lax
from jax.experimental import pallas as pl
from jax.experimental.pallas import tpu as pltpu
from jax.sharding import Mesh, PartitionSpec as P

NPIX = 4096
PASS = 512
SHIFT = 64
LEVELS = 4
SOURCES = 4
BAKE = 4
Z = 2
PUPIL_TILES = (PASS + 2 * SHIFT) // 8
DIFF_ACID = 0.12
DIFF_QUENCH = 0.04
QUENCH_RATE = 0.6
CATALYSIS = 0.4

DEVICES = 128
ROWS = NPIX // DEVICES
OWNERS = 32
FREQS = PASS // OWNERS
WIDE = 2 * FREQS
HALO = 4
TALL = 144
BRICK_ROWS = 128
BRICK_COLS = 1024
EXT_ROWS = BRICK_ROWS + 2 * HALO
EXT_COLS = BRICK_COLS + 128
COL_TILES = EXT_COLS // 128
EARLY = 2
ALL = ("zl", "c", "y", "zh", "x")
MIB = 1024 * 1024
PARTS = 4


def cos_sin(first, second):
    theta = (np.mod(first[:, None] * second[None, :], NPIX)).astype(np.float32)
    theta = (theta * np.float32(2.0 * math.pi / NPIX)).astype(np.float64)
    return np.cos(theta).astype(np.float32), np.sin(theta).astype(np.float32)


def bf16(table):
    return table.astype(jnp.bfloat16)


FREQ = np.arange(PASS, dtype=np.int64) - PASS // 2
HALF = PASS // 2


def forward_columns():
    return bf16(np.concatenate(cos_sin(np.arange(NPIX), np.arange(HALF)), axis=1))


def forward_rows():
    order = np.arange(NPIX).reshape(2, 2, DEVICES // 4, 2, 16).transpose(1, 3, 0, 2, 4).reshape(NPIX)
    both = np.concatenate(cos_sin(np.arange(HALF), order), axis=0)
    return bf16(both.reshape(PASS, 2, 2, NPIX // 4).transpose(1, 2, 0, 3))


def edge_columns():
    cosine, sine = cos_sin(np.array([HALF]), np.arange(128))
    return np.asarray(bf16(np.concatenate([cosine, sine], axis=0))).astype(np.float32)


def edge_rows():
    cosine, sine = cos_sin(np.array([HALF]), np.arange(16))
    both = np.repeat(np.stack([cosine.reshape(16, 1), sine.reshape(16, 1)]), 128, axis=2)
    return np.asarray(bf16(both)).astype(np.float32)


def inverse_rows(tiles):
    blocks = []
    for tile in range(tiles):
        local = np.arange(TALL)
        local = np.where(local < BRICK_ROWS + HALO, local, local - EXT_ROWS)
        pixels = np.mod(tile * BRICK_ROWS + local, NPIX)
        cosine, sine = cos_sin(pixels, FREQ)
        upper = np.concatenate([cosine, -sine], axis=1)
        lower = np.concatenate([sine, cosine], axis=1)
        blocks.append(np.concatenate([upper, lower], axis=0))
    return bf16(np.stack(blocks))


def inverse_cols(sources):
    lanes = np.arange(EXT_COLS)
    local = np.where(lanes < BRICK_COLS + 64, lanes, lanes - EXT_COLS)
    blocks = []
    for source in range(sources):
        pixels = np.mod(source * BRICK_COLS + local, NPIX)
        cosine, sine = cos_sin(FREQ, pixels)
        real = np.concatenate([cosine, -sine], axis=0).reshape(2 * PASS, COL_TILES, 1, 128)
        imag = np.concatenate([sine, cosine], axis=0).reshape(2 * PASS, COL_TILES, 1, 128)
        both = np.concatenate([real, imag], axis=2).reshape(2 * PASS, COL_TILES, 256)
        blocks.append(both.transpose(1, 0, 2))
    return bf16(np.stack(blocks))


def lane_ids(shape):
    return lax.broadcasted_iota(jnp.int32, shape, len(shape) - 1)


def columns_kernel(trans_ref, ids_hbm, table_hbm, edge_ref, out_ref, ids_ref, table_ref, perm_ref, sems):
    depth = NPIX // PARTS
    copies = []
    for k in range(PARTS):
        part = pl.ds(k * depth, depth)
        both = (
            pltpu.make_async_copy(ids_hbm.at[:, part], ids_ref.at[:, part], sems.at[0, k]),
            pltpu.make_async_copy(table_hbm.at[part], table_ref.at[part], sems.at[1, k]),
        )
        for copy in both:
            copy.start()
        copies.append(both)
    source = lax.broadcasted_iota(jnp.int32, (PASS, PASS), 0)
    lane = lax.broadcasted_iota(jnp.int32, (PASS, PASS), 1)
    plane, place = lane // FREQS % 2, lane // WIDE * FREQS + lane % FREQS
    perm_ref[0] = (source == plane * HALF + (HALF - place) % HALF).astype(jnp.float32).astype(jnp.bfloat16)
    perm_ref[1] = (source == plane * HALF + place).astype(jnp.float32).astype(jnp.bfloat16)
    acc = jnp.zeros((2 * ROWS, PASS), jnp.float32)
    total = jnp.zeros((2 * ROWS, 128), jnp.float32)
    for k in range(PARTS):
        part = slice(k * depth, k * depth + depth)
        copies[k][0].wait()
        ids = ids_ref[:, part]
        planes = []
        for plane in range(2):
            value = jnp.zeros(ids.shape, jnp.float32)
            for level in range(LEVELS):
                value = jnp.where(ids == level, trans_ref[plane, level], value)
            planes.append(value)
        trans = jnp.concatenate(planes, axis=0).astype(jnp.bfloat16)
        exact = trans.astype(jnp.float32)
        for tile in range(depth // 128):
            total = total + exact[:, 128 * tile : 128 * tile + 128]
        copies[k][1].wait()
        acc = acc + jnp.dot(trans, table_ref[part, :], preferred_element_type=jnp.float32)
    edge_cos = jnp.sum(total * edge_ref[0:1, :], axis=1, keepdims=True)
    edge_sin = jnp.sum(total * edge_ref[1:2, :], axis=1, keepdims=True)
    cos_real, cos_imag = acc[:ROWS, :HALF], acc[ROWS:, :HALF]
    sin_real, sin_imag = acc[:ROWS, HALF:], acc[ROWS:, HALF:]
    first = lane_ids((ROWS, HALF)) == 0
    low_real = jnp.where(first, edge_cos[:ROWS] - edge_sin[ROWS:], cos_real - sin_imag)
    low_imag = jnp.where(first, edge_cos[ROWS:] + edge_sin[:ROWS], cos_imag + sin_real)
    low = jnp.concatenate([low_real, low_imag], axis=1).astype(jnp.bfloat16)
    high = jnp.concatenate([cos_real + sin_imag, cos_imag - sin_real], axis=1).astype(jnp.bfloat16)
    sides = [
        jnp.dot(low, perm_ref[0], preferred_element_type=jnp.float32),
        jnp.dot(high, perm_ref[1], preferred_element_type=jnp.float32),
    ]
    group = lane_ids((16, 128)) // WIDE
    for y in range(4):
        for x in range(4):
            owner = y * 4 + x
            chunk = jnp.zeros((16, 128), jnp.float32)
            for g in range(4):
                q, side = g // 2, g % 2
                major = owner // 4 * 128
                piece = sides[side][16 * q : 16 * q + 16, major : major + 128]
                turn = (g - owner) % 4 * WIDE
                piece = pltpu.roll(piece, turn, 1) if turn else piece
                chunk = jnp.where(group == g, piece, chunk)
            value = chunk.astype(jnp.bfloat16)
            for plane_z in range(4):
                dest = plane_z // 2 * 32 + y * 8 + plane_z % 2 * 4 + x
                out_ref[16 * dest : 16 * dest + 16, :] = value


def columns_call(trans_table, mask_ids, table, edge):
    vmem = pl.BlockSpec(memory_space=pltpu.VMEM)
    hbm = pl.BlockSpec(memory_space=pl.ANY)
    return pl.pallas_call(
        columns_kernel,
        out_shape=jax.ShapeDtypeStruct((DEVICES // 2 * 16, 128), jnp.bfloat16),
        in_specs=[pl.BlockSpec(memory_space=pltpu.SMEM), hbm, hbm, vmem],
        out_specs=vmem,
        scratch_shapes=[
            pltpu.VMEM((ROWS, NPIX), jnp.int32),
            pltpu.VMEM((NPIX, PASS), jnp.bfloat16),
            pltpu.VMEM((2, PASS, PASS), jnp.bfloat16),
            pltpu.SemaphoreType.DMA((2, PARTS)),
        ],
        compiler_params=pltpu.CompilerParams(vmem_limit_bytes=56 * MIB),
        name="columns",
    )(trans_table, mask_ids, table, edge)


def spectrum_kernel(core_ref, table_hbm, cols_ref, edge_ref, keep_ref, send_ref, table_ref, block_ref, sems):
    core = core_ref[0]
    copies = []
    for q in range(2):
        copies.append(pltpu.make_async_copy(table_hbm.at[core, q], table_ref.at[q], sems.at[q]))
        copies[q].start()
    columns = cols_ref[...].astype(jnp.float32)
    total = [columns[16 * k : 16 * k + 16] for k in range(DEVICES // 2)]
    while len(total) > 1:
        total = [a + b for a, b in zip(total[::2], total[1::2])]
    edge_cos = jnp.sum(total[0] * edge_ref[0], axis=0, keepdims=True)
    edge_sin = jnp.sum(total[0] * edge_ref[1], axis=0, keepdims=True)

    def turn(value):
        is_real = lane_ids(value.shape) % WIDE < FREQS
        return jnp.where(is_real, pltpu.roll(value, 128 - FREQS, 1), -pltpu.roll(value, FREQS, 1))

    edges = jnp.concatenate([edge_cos, edge_sin, jnp.zeros((6, 128), jnp.float32)], axis=0)
    edges = edges + pltpu.roll(edges, 64, 1)
    edge = edges[0:1] - turn(edges)[1:2]
    source = lax.broadcasted_iota(jnp.int32, (HALF, HALF), 0)
    place = lax.broadcasted_iota(jnp.int32, (HALF, HALF), 1)
    perm = (source == (HALF - place) % HALF).astype(jnp.float32).astype(jnp.bfloat16)
    products = []
    for q in range(2):
        copies[q].wait()
        products.append(jnp.dot(table_ref[q], cols_ref[...], preferred_element_type=jnp.float32))
    folded = jnp.where(lane_ids((PASS, 128)) < 64, products[0], products[1])
    folded = folded + pltpu.roll(folded, 64, 1)
    cosine, turned = folded[:HALF], turn(folded[HALF:])
    first = lax.broadcasted_iota(jnp.int32, cosine.shape, 0) == 0
    scale = 1.0 / (NPIX * NPIX)
    high = jnp.transpose((cosine + turned) * scale)[: 2 * WIDE]
    low = jnp.transpose(jnp.where(first, edge, cosine - turned) * scale)[: 2 * WIDE]
    pieces = []
    rest = low
    for _ in range(3):
        piece = rest.astype(jnp.bfloat16)
        rest = rest - piece.astype(jnp.float32)
        pieces.append(jnp.dot(piece, perm, preferred_element_type=jnp.float32))
    block_ref[:, :HALF] = pieces[0] + pieces[1] + pieces[2]
    block_ref[:, HALF:] = high
    keep_ref[...] = block_ref[pl.ds(pl.multiple_of(core * WIDE, WIDE), WIDE), :]
    send_ref[...] = block_ref[pl.ds(pl.multiple_of((1 - core) * WIDE, WIDE), WIDE), :]


def spectrum_call(core, table, cols, edge):
    vmem = pl.BlockSpec(memory_space=pltpu.VMEM)
    part = jax.ShapeDtypeStruct((WIDE, PASS), jnp.float32)
    return pl.pallas_call(
        spectrum_kernel,
        out_shape=(part, part),
        in_specs=[pl.BlockSpec(memory_space=pltpu.SMEM), pl.BlockSpec(memory_space=pl.ANY), vmem, vmem],
        out_specs=(vmem, vmem),
        scratch_shapes=[
            pltpu.VMEM(table.shape[1:], jnp.bfloat16),
            pltpu.VMEM((2 * WIDE, PASS), jnp.float32),
            pltpu.SemaphoreType.DMA((2,)),
        ],
        compiler_params=pltpu.CompilerParams(vmem_limit_bytes=50 * MIB),
        name="spectrum",
    )(core, table, cols, edge)


def spread_kernel(keep_ref, come_ref, out_ref):
    block = keep_ref[...] + come_ref[...]
    for dest in range(16):
        out_ref[dest * WIDE : (dest + 1) * WIDE, :] = block


def spread_call(keep, come):
    vmem = pl.BlockSpec(memory_space=pltpu.VMEM)
    return pl.pallas_call(
        spread_kernel,
        out_shape=jax.ShapeDtypeStruct((16 * WIDE, PASS), jnp.float32),
        in_specs=[vmem, vmem],
        out_specs=vmem,
        compiler_params=pltpu.CompilerParams(vmem_limit_bytes=6 * MIB),
        name="spread",
    )(keep, come)


def pack_kernel(shifts_ref, weights_ref, pupil_ref, dose_ref, turned_ref, last_ref, first_ref, note_ref):
    blocks = pupil_ref.shape[1] // 128
    for plane in range(2):
        for i in range(blocks):
            for j in range(blocks):
                piece = pupil_ref[plane, 128 * i : 128 * i + 128, 128 * j : 128 * j + 128]
                turned_ref[plane, 128 * j : 128 * j + 128, 128 * i : 128 * i + 128] = jnp.transpose(piece)

    def note(shape):
        lane = lane_ids(shape)
        shift_x, shift_y = shifts_ref[0, 0].astype(jnp.float32), shifts_ref[0, 1].astype(jnp.float32)
        return jnp.where(lane == 64, shift_x, jnp.where(lane == 65, shift_y, weights_ref[0]))

    lane = lane_ids((BRICK_ROWS, 128))
    middle = (lane >= 64) & (lane < 67)
    for z in range(Z):
        last_ref[z] = jnp.where(middle, note((BRICK_ROWS, 128)), dose_ref[z, :, BRICK_COLS - 128 :])
        first_ref[z] = jnp.where(middle, note((BRICK_ROWS, 128)), dose_ref[z, :, :128])
    note_ref[...] = note((8, 128))


def pack_call(shifts, weights, pupil, dose):
    vmem = pl.BlockSpec(memory_space=pltpu.VMEM)
    smem = pl.BlockSpec(memory_space=pltpu.SMEM)
    side = jax.ShapeDtypeStruct((Z, BRICK_ROWS, 128), jnp.float32)
    return pl.pallas_call(
        pack_kernel,
        out_shape=(
            jax.ShapeDtypeStruct(pupil.shape, jnp.float32),
            side,
            side,
            jax.ShapeDtypeStruct((8, 128), jnp.float32),
        ),
        in_specs=[smem, smem, vmem, vmem],
        out_specs=(vmem,) * 4,
        compiler_params=pltpu.CompilerParams(vmem_limit_bytes=12 * MIB),
        cost_estimate=pl.CostEstimate(flops=1_000_000, bytes_accessed=9_000_000, transcendentals=0),
        name="pack",
    )(shifts, weights, pupil, dose)


def edge_kernel(dose_ref, before_ref, after_ref, side_ref, last_ref, first_ref):
    lane = lane_ids((BRICK_ROWS, 128))
    for z in range(Z):
        side = jnp.where(lane < 64, after_ref[z], before_ref[z])
        side_ref[z] = side
        last_ref[z, :, :BRICK_COLS] = dose_ref[z, BRICK_ROWS - 8 :, :]
        last_ref[z, :, BRICK_COLS:] = side[BRICK_ROWS - 8 :]
        first_ref[z, :, :BRICK_COLS] = dose_ref[z, :8, :]
        first_ref[z, :, BRICK_COLS:] = side[:8]


def edge_call(dose, before, after):
    vmem = pl.BlockSpec(memory_space=pltpu.VMEM)
    row = jax.ShapeDtypeStruct((Z, 8, EXT_COLS), jnp.float32)
    return pl.pallas_call(
        edge_kernel,
        out_shape=(jax.ShapeDtypeStruct((Z, BRICK_ROWS, 128), jnp.float32), row, row),
        in_specs=[vmem] * 3,
        out_specs=(vmem,) * 3,
        compiler_params=pltpu.CompilerParams(vmem_limit_bytes=6 * MIB),
        cost_estimate=pl.CostEstimate(flops=1_000_000, bytes_accessed=2_000_000, transcendentals=0),
        name="edge",
    )(dose, before, after)


def window_kernel(shifts_ref, turned_ref, out_hbm, token_ref, out_ref, sems):
    token_ref[...] = jnp.zeros_like(token_ref)
    lane = lane_ids((8, 128))
    row = lax.broadcasted_iota(jnp.int32, (8, 128), 0)
    zero = jnp.zeros((8, 128), jnp.float32)
    tiles, group, groups = PASS // 8, 13, 4
    edge = SHIFT * 2 // 8

    def source_step(s, carry):
        lift = SHIFT - shifts_ref[s, 1]
        shift = SHIFT - shifts_ref[s, 0]
        first, rest = lift // 8, lax.rem(lift, 8)
        rise = lax.rem(8 - rest, 8)
        turn = lax.rem(256 - shift, 128)
        keep_lane = lane < 128 - shift
        keep_row = row < 8 - rest
        begin = jnp.minimum(edge - first - jnp.where(rest > 0, 1, 0), tiles - group * groups)

        def clear(t, inner):
            for plane in range(2):
                for v in range(4):
                    out_ref[2 * s + plane, pl.ds(pl.multiple_of(t * 8, 8), 8), 128 * v : 128 * v + 128] = zero
            return inner

        lax.fori_loop(0, begin, clear, 0)
        lax.fori_loop(begin + group * groups, tiles, clear, 0)

        def block(t, inner):
            start = begin + t * group
            for plane in range(2):
                before = None
                for k in range(group + 1):
                    tile = jnp.minimum(start + k + first, PUPIL_TILES - 1)
                    base = pl.ds(pl.multiple_of(tile * 8, 8), 8)
                    turned = [zero] + [
                        pltpu.roll(turned_ref[plane, base, 128 * v : 128 * v + 128], turn, 1) for v in range(1, 5)
                    ]
                    cut = [jnp.where(keep_lane, turned[v], turned[v + 1]) for v in range(4)]
                    after = [pltpu.roll(c, rise, 0) for c in cut]
                    if before is not None:
                        place = pl.ds(pl.multiple_of((start + k - 1) * 8, 8), 8)
                        for v in range(4):
                            value = jnp.where(keep_row, before[v], after[v])
                            out_ref[2 * s + plane, place, 128 * v : 128 * v + 128] = value
                    before = after
            return inner

        lax.fori_loop(0, groups, block, 0)
        leave(s).start()
        return carry

    def leave(s):
        planes = pl.ds(2 * s, 2)
        return pltpu.make_async_copy(out_ref.at[planes], out_hbm.at[planes], sems.at[s])

    lax.fori_loop(0, SOURCES, source_step, 0)
    for s in range(SOURCES):
        leave(s).wait()


def window_call(shifts, pupil):
    vmem = pl.BlockSpec(memory_space=pltpu.VMEM)
    planes = 2 * SOURCES
    return pl.pallas_call(
        window_kernel,
        out_shape=(
            jax.ShapeDtypeStruct((3 * planes, PASS, PASS), jnp.float32),
            jax.ShapeDtypeStruct((8, 128), jnp.float32),
        ),
        in_specs=[pl.BlockSpec(memory_space=pltpu.SMEM), vmem],
        out_specs=(pl.BlockSpec(memory_space=pl.ANY), vmem),
        scratch_shapes=[pltpu.VMEM((planes, PASS, PASS), jnp.float32), pltpu.SemaphoreType.DMA((SOURCES,))],
        compiler_params=pltpu.CompilerParams(vmem_limit_bytes=44 * MIB),
        cost_estimate=pl.CostEstimate(flops=10_000_000, bytes_accessed=11_000_000, transcendentals=0),
        name="window",
    )(shifts, pupil)


def rowfield_half(s, spec_ref, window_ref, rows_ref, filt_ref):
    slot = s % 2

    def block(o, inner):
        base = pl.multiple_of(o * WIDE, WIDE)
        place = pl.ds(pl.multiple_of(o * FREQS, FREQS), FREQS)
        real = spec_ref[pl.ds(base, FREQS), :]
        imag = spec_ref[pl.ds(base + FREQS, FREQS), :]
        w_real = window_ref[2 * s, place, :]
        w_imag = window_ref[2 * s + 1, place, :]
        filt_ref[slot, place, :PASS] = (w_real * real - w_imag * imag).astype(jnp.bfloat16)
        filt_ref[slot, place, PASS:] = (w_real * imag + w_imag * real).astype(jnp.bfloat16)
        return inner

    lax.fori_loop(0, 16, block, 0, unroll=16)
    return lax.dot_general(
        rows_ref[...], filt_ref[slot], (((1,), (1,)), ((), ())), preferred_element_type=jnp.float32
    ).astype(jnp.bfloat16)


def own_kernel(
    where_ref, token_ref, own_ref, window_hbm, rows_hbm, dose_hbm,
    field_ref, rows_ref, other_ref, dose_ref, window_ref, filt_ref, sems,
):
    core = where_ref[0]
    mine = pl.ds(pl.multiple_of(core * HALF, HALF), HALF)
    theirs = pl.ds(pl.multiple_of((1 - core) * HALF, HALF), HALF)
    rows_copy = pltpu.make_async_copy(rows_hbm.at[where_ref[1]], rows_ref, sems.at[0])
    rows_copy.start()
    copies = []
    for s in range(SOURCES):
        planes = pl.ds(2 * s, 2)
        copies.append(pltpu.make_async_copy(window_hbm.at[planes, mine], window_ref.at[planes], sems.at[1 + s]))
        copies[s].start()
    later = [
        pltpu.make_async_copy(dose_hbm, dose_ref, sems.at[1 + SOURCES]),
        pltpu.make_async_copy(window_hbm.at[pl.ds(0, 2 * SOURCES), theirs], other_ref, sems.at[2 + SOURCES]),
    ]
    for copy in later:
        copy.start()
    rows_copy.wait()
    for s in range(SOURCES):
        if s % 2 == 0:
            copies[s].wait()
            copies[s + 1].wait()
        rowfield = rowfield_half(s, own_ref, window_ref, rows_ref, filt_ref)
        field_ref[s * TALL : (s + 1) * TALL, :HALF] = rowfield[:TALL]
        field_ref[s * TALL : (s + 1) * TALL, HALF:] = rowfield[TALL:]
    for copy in later:
        copy.wait()


def own_call(where, token, own, window, rows, dose):
    smem = pl.BlockSpec(memory_space=pltpu.SMEM)
    vmem = pl.BlockSpec(memory_space=pltpu.VMEM)
    hbm = pl.BlockSpec(memory_space=pl.ANY)
    half = (2 * SOURCES, HALF, PASS)
    return pl.pallas_call(
        own_kernel,
        out_shape=(
            jax.ShapeDtypeStruct((SOURCES * TALL, PASS), jnp.bfloat16),
            jax.ShapeDtypeStruct(rows.shape[1:], jnp.bfloat16),
            jax.ShapeDtypeStruct(half, jnp.float32),
            jax.ShapeDtypeStruct(dose.shape, jnp.float32),
        ),
        in_specs=[smem, hbm, vmem, hbm, hbm, hbm],
        out_specs=(vmem,) * 4,
        scratch_shapes=[
            pltpu.VMEM(half, jnp.float32),
            pltpu.VMEM((2, HALF, 2 * PASS), jnp.bfloat16),
            pltpu.SemaphoreType.DMA((3 + SOURCES,)),
        ],
        compiler_params=pltpu.CompilerParams(vmem_limit_bytes=36 * MIB),
        cost_estimate=pl.CostEstimate(flops=10_000_000, bytes_accessed=9_000_000, transcendentals=0),
        name="own_half",
    )(where, token, own, window, rows, dose)


def resist_kernel(
    where_ref, weights_ref, quencher_ref, half_ref, other_ref, window_ref, rows_ref, cols_hbm,
    dose_ref, side_ref, above_ref, below_ref, acid_hbm, inhibitor_hbm,
    cols_ref, filt_ref, field_ref, a_ref, b_ref, p_ref, q_ref, sum_ref, acid_ref, inhibitor_ref, sems, out_sems,
):
    core = where_ref[0]
    cols_copies = []
    for k, (begin, count) in enumerate(((0, EARLY), (EARLY, COL_TILES - EARLY))):
        part = pl.ds(begin, count)
        cols_copies.append(pltpu.make_async_copy(cols_hbm.at[where_ref[2], part], cols_ref.at[part], sems.at[k]))
        cols_copies[k].start()
    mine = pl.multiple_of(core * HALF, HALF)
    theirs = pl.multiple_of((1 - core) * HALF, HALF)
    field_ref[:, pl.ds(mine, HALF)] = half_ref[:, :HALF]
    field_ref[:, pl.ds(PASS + mine, HALF)] = half_ref[:, HALF:]
    for s in range(SOURCES):
        rowfield = rowfield_half(s, other_ref, window_ref, rows_ref, filt_ref)
        field_ref[s * TALL : (s + 1) * TALL, pl.ds(theirs, HALF)] = rowfield[:TALL]
        field_ref[s * TALL : (s + 1) * TALL, pl.ds(PASS + theirs, HALF)] = rowfield[TALL:]
    cols_copies[0].wait()
    row_of = lax.broadcasted_iota(jnp.int32, (8, 128), 0)

    for b in range(COL_TILES):
        if b == EARLY:
            cols_copies[1].wait()
        field = jnp.dot(field_ref[...], cols_ref[b], preferred_element_type=jnp.float32)
        intensity = jnp.zeros((EXT_ROWS, 128), jnp.float32)
        for s in range(SOURCES):
            part = field[s * TALL : s * TALL + EXT_ROWS]
            real, imag = part[:, :128], part[:, 128:]
            intensity = intensity + weights_ref[s] * (real * real + imag * imag)
        lanes = slice(b * 128, b * 128 + 128)
        for z in range(Z):
            bottom = jnp.where(row_of < HALO, below_ref[z, :, lanes], above_ref[z, :, lanes])
            middle = dose_ref[z, :, lanes] if b < COL_TILES - 1 else side_ref[z]
            a_ref[z, :BRICK_ROWS, lanes] = QUENCH_RATE - QUENCH_RATE * jnp.exp(-middle * intensity[:BRICK_ROWS])
            a_ref[z, BRICK_ROWS:, lanes] = QUENCH_RATE - QUENCH_RATE * jnp.exp(-bottom * intensity[BRICK_ROWS:])

    tiles = EXT_ROWS // 8
    row_id = lax.broadcasted_iota(jnp.int32, (8, EXT_COLS), 0)
    quench = [QUENCH_RATE * quencher_ref[0], QUENCH_RATE * quencher_ref[1]]

    def neighbours(ref, z, t):
        here = ref[z, 8 * t : 8 * t + 8, :]
        up, down = (t - 1) % tiles, (t + 1) % tiles
        above = pltpu.roll(jnp.where(row_id == 7, ref[z, 8 * up : 8 * up + 8, :], here), 1, 0)
        below = pltpu.roll(jnp.where(row_id == 0, ref[z, 8 * down : 8 * down + 8, :], here), 7, 0)
        left = pltpu.roll(here, 1, 1)
        right = pltpu.roll(here, EXT_COLS - 1, 1)
        return here, (above + below) + (left + right)

    buffers = [(a_ref, b_ref), (b_ref, a_ref), (a_ref, b_ref), (b_ref, None)]
    quenches = [(None, p_ref), (p_ref, q_ref), (q_ref, p_ref), (p_ref, None)]
    copies = []
    for step in range(BAKE):
        old, new = buffers[step]
        q_old, q_new = quenches[step]
        for t in range(tiles if new is not None else BRICK_ROWS // 8):
            rows = slice(8 * t, 8 * t + 8)
            acid = [neighbours(old, z, t) for z in range(Z)]
            acid_z = acid[0][0] + acid[1][0]
            if q_old is None:
                quench_here = quench
                quench_sum = [4.0 * quench[z] for z in range(Z)]
            elif q_new is None:
                quench_here = [q_old[z, rows, :] for z in range(Z)]
            else:
                pairs = [neighbours(q_old, z, t) for z in range(Z)]
                quench_here = [pair[0] for pair in pairs]
                quench_sum = [pair[1] for pair in pairs]
            quench_z = quench_here[0] + quench_here[1]
            for z in range(Z):
                here, around = acid[z]
                reaction = here * quench_here[z]
                fresh = ((1.0 - 6.0 * DIFF_ACID) * here + DIFF_ACID * (around + acid_z)) - reaction
                if new is not None:
                    new[z, rows, :] = fresh
                else:
                    acid_ref[z, rows, :] = fresh[:, :BRICK_COLS] * (1.0 / QUENCH_RATE)
                if q_new is not None:
                    kept = (1.0 - 6.0 * DIFF_QUENCH) * quench_here[z]
                    q_new[z, rows, :] = (kept + DIFF_QUENCH * (quench_sum[z] + quench_z)) - reaction
                if t < BRICK_ROWS // 8:
                    if step == 0:
                        sum_ref[z, rows, :] = here[:, :BRICK_COLS]
                    elif new is not None:
                        sum_ref[z, rows, :] = sum_ref[z, rows, :] + here[:, :BRICK_COLS]
                    else:
                        total = sum_ref[z, rows, :] + here[:, :BRICK_COLS]
                        inhibitor_ref[z, rows, :] = jnp.exp((-CATALYSIS / QUENCH_RATE) * total)
            if new is None and t % 4 == 3:
                ready = pl.ds(8 * (t - 3), 32)
                for k, (near, far) in enumerate(((acid_ref, acid_hbm), (inhibitor_ref, inhibitor_hbm))):
                    copy = pltpu.make_async_copy(near.at[:, ready], far.at[:, ready], out_sems.at[t // 4, k])
                    copy.start()
                    copies.append(copy)
    for copy in copies:
        copy.wait()


def resist_call(where, weights, quencher, half, other, window, rows, cols, dose, side, above, below):
    smem = pl.BlockSpec(memory_space=pltpu.SMEM)
    vmem = pl.BlockSpec(memory_space=pltpu.VMEM)
    hbm = pl.BlockSpec(memory_space=pl.ANY)
    brick_shape = (Z, BRICK_ROWS, BRICK_COLS)
    out = jax.ShapeDtypeStruct(brick_shape, jnp.float32)
    brick = pltpu.VMEM((Z, EXT_ROWS, EXT_COLS), jnp.float32)
    near = pltpu.VMEM(brick_shape, jnp.float32)
    return pl.pallas_call(
        resist_kernel,
        out_shape=(out, out),
        in_specs=[smem] * 3 + [vmem] * 4 + [hbm] + [vmem] * 4,
        out_specs=(hbm, hbm),
        scratch_shapes=[
            pltpu.VMEM(cols.shape[1:], jnp.bfloat16),
            pltpu.VMEM((2, HALF, 2 * PASS), jnp.bfloat16),
            pltpu.VMEM((SOURCES * TALL, 2 * PASS), jnp.bfloat16),
            brick, brick, brick, brick,
            near, near, near,
            pltpu.SemaphoreType.DMA((2,)),
            pltpu.SemaphoreType.DMA((4, 2)),
        ],
        compiler_params=pltpu.CompilerParams(vmem_limit_bytes=46 * MIB),
        name="resist",
    )(where, weights, quencher, half, other, window, rows, cols, dose, side, above, below)


def ring(axes, step):
    size = lax.axis_size(axes)
    return [(i, (i + step) % size) for i in range(size)]


def body(mask_ids, trans_table, pupil, shifts, weights, dose, quencher):
    src_axes, tile_axes = ("zl", "c"), ("y", "zh", "x")
    core, src, tile = lax.axis_index("c"), lax.axis_index(src_axes), lax.axis_index(tile_axes)
    packed = columns_call(trans_table, mask_ids, jnp.asarray(forward_columns()), jnp.asarray(edge_columns()))
    packed, shifts, weights, dose_late, pupil = lax.optimization_barrier((packed, shifts, weights, dose, pupil))
    cols = lax.all_to_all(packed, ("zl", "y", "zh", "x"), 0, 0, tiled=True)

    turned, last, first, note = pack_call(shifts, weights, pupil, dose_late)
    cols, turned, last, first, note = lax.optimization_barrier((cols, turned, last, first, note))
    before = lax.ppermute(last, src_axes, ring(src_axes, 1))
    after = lax.ppermute(first, src_axes, ring(src_axes, -1))
    far = lax.ppermute(note, src_axes, ring(src_axes, 2))
    notes = [note[:1, 64:67], far[:1, 64:67], before[0, :1, 64:67], after[0, :1, 64:67]]
    sources = jnp.concatenate(notes, axis=0)
    all_shifts, all_weights = sources[:, :2].astype(jnp.int32), sources[:, 2]
    side, last, first = edge_call(dose_late, before, after)
    above = lax.ppermute(last, tile_axes, ring(tile_axes, 1))
    below = lax.ppermute(first, tile_axes, ring(tile_axes, -1))
    where = jnp.stack([core, tile, src]).astype(jnp.int32)

    swap = [(0, 1), (1, 0)]
    core_ref = core.reshape(1).astype(jnp.int32)
    keep, send = spectrum_call(core_ref, jnp.asarray(forward_rows()), cols, jnp.asarray(edge_rows()))
    block = spread_call(keep, lax.ppermute(send, "c", swap))
    own = lax.all_to_all(block, ("y", "x"), 0, 0, tiled=True)
    window, token = window_call(all_shifts, turned)
    own, token, all_weights, side, above, below, where = lax.optimization_barrier(
        (own, token, all_weights, side, above, below, where)
    )
    other = lax.ppermute(own, "c", swap)
    half, row_table, window_other, dose_near = own_call(where, token, own, window, jnp.asarray(inverse_rows(32)), dose)
    return resist_call(
        where, all_weights, quencher, half, other, window_other, row_table,
        jnp.asarray(inverse_cols(4)), dose_near, side, above, below,
    )


def solution(mesh):
    parts = Mesh(mesh.devices.reshape(2, 2, 4, 2, 4), ALL)
    src, tile = ("zl", "c"), ("y", "zh", "x")
    inner = jax.shard_map(
        body,
        mesh=parts,
        in_specs=(
            P(ALL, None),
            P(),
            P(),
            P(src, None),
            P(src),
            P(None, tile, src),
            P(),
        ),
        out_specs=(P(None, tile, src), P(None, tile, src)),
        check_vma=False,
    )
    return inner
```

```python
import math

import jax
import jax.numpy as jnp
import numpy as np
from jax import lax
from jax.experimental import pallas as pl
from jax.experimental.pallas import tpu as pltpu
from jax.sharding import Mesh, PartitionSpec as P

NPIX = 4096
PASS = 512
SHIFT = 64
LEVELS = 4
SOURCES = 4
BAKE = 4
Z = 2
PUPIL_TILES = (PASS + 2 * SHIFT) // 8
DIFF_ACID = 0.12
DIFF_QUENCH = 0.04
QUENCH_RATE = 0.6
CATALYSIS = 0.4

DEVICES = 128
ROWS = NPIX // DEVICES
OWNERS = 32
FREQS = PASS // OWNERS
WIDE = 2 * FREQS
HALO = 4
TALL = 144
BRICK_ROWS = 128
BRICK_COLS = 1024
EXT_ROWS = BRICK_ROWS + 2 * HALO
EXT_COLS = BRICK_COLS + 128
COL_TILES = EXT_COLS // 128
EARLY = 2
ALL = ("zl", "c", "y", "zh", "x")
MIB = 1024 * 1024
QUARTER = NPIX // 4


def cos_sin(first, second):
    theta = (np.mod(first[:, None] * second[None, :], NPIX)).astype(np.float32)
    theta = (theta * np.float32(2.0 * math.pi / NPIX)).astype(np.float64)
    return np.cos(theta).astype(np.float32), np.sin(theta).astype(np.float32)


def bf16(table):
    return np.asarray(table).astype(jnp.bfloat16)


FREQ = np.arange(PASS, dtype=np.int64) - PASS // 2
HALF = PASS // 2


def forward_columns():
    return bf16(np.concatenate(cos_sin(np.arange(QUARTER), np.arange(HALF)), axis=1))


def forward_rows():
    order = np.arange(2 * QUARTER).reshape(2, DEVICES // 4, 2, 16).transpose(0, 2, 1, 3).reshape(2 * QUARTER)
    both = np.concatenate(cos_sin(np.arange(HALF), order), axis=0)
    table = both.reshape(PASS, 2, 2, QUARTER // 2).transpose(1, 2, 0, 3)
    return bf16(np.pad(table, ((0, 0), (0, 14), (0, 0), (0, 0))))


def edge_values(place):
    tables = [bf16(part)[0] for part in cos_sin(np.array([HALF]), np.arange(16))]
    results = []
    for table in tables:
        value = jnp.zeros(place.shape, jnp.float32)
        for k in range(16):
            value = jnp.where(place == k, float(table[k]), value)
        results.append(value)
    return results


def inverse_rows(tiles):
    blocks = []
    for tile in range(tiles):
        local = np.arange(TALL)
        local = np.where(local < BRICK_ROWS + HALO, local, local - EXT_ROWS)
        pixels = np.mod(tile * BRICK_ROWS + local, NPIX)
        cosine, sine = cos_sin(pixels, FREQ)
        upper = np.concatenate([cosine, -sine], axis=1)
        lower = np.concatenate([sine, cosine], axis=1)
        blocks.append(np.concatenate([upper, lower], axis=0))
    return bf16(np.stack(blocks))


def inverse_cols(sources):
    lanes = np.arange(EXT_COLS)
    local = np.where(lanes < BRICK_COLS + 64, lanes, lanes - EXT_COLS)
    blocks = []
    for source in range(sources):
        pixels = np.mod(source * BRICK_COLS + local, NPIX)
        cosine, sine = cos_sin(FREQ, pixels)
        real = np.concatenate([cosine, -sine], axis=0).reshape(2 * PASS, COL_TILES, 1, 128)
        imag = np.concatenate([sine, cosine], axis=0).reshape(2 * PASS, COL_TILES, 1, 128)
        both = np.concatenate([real, imag], axis=2).reshape(2 * PASS, COL_TILES, 256)
        blocks.append(both.transpose(1, 0, 2))
    return bf16(np.stack(blocks))


def lane_ids(shape):
    return lax.broadcasted_iota(jnp.int32, shape, len(shape) - 1)


def columns_kernel(trans_ref, ids_hbm, table_hbm, out_ref, ids_ref, table_ref, pixels_ref, perm_ref, sems):
    ids_copy = pltpu.make_async_copy(ids_hbm, ids_ref, sems.at[0])
    table_copy = pltpu.make_async_copy(table_hbm, table_ref, sems.at[1])
    ids_copy.start()
    table_copy.start()
    source = lax.broadcasted_iota(jnp.int32, (PASS, PASS), 0)
    lane = lax.broadcasted_iota(jnp.int32, (PASS, PASS), 1)
    plane, place = lane // FREQS % 2, lane // WIDE * FREQS + lane % FREQS
    perm_ref[0] = (source == plane * HALF + (HALF - place) % HALF).astype(jnp.float32).astype(jnp.bfloat16)
    perm_ref[1] = (source == plane * HALF + place).astype(jnp.float32).astype(jnp.bfloat16)
    ids_copy.wait()
    total = jnp.zeros((2 * ROWS, 128), jnp.float32)
    for m in range(4):
        ids = ids_ref[:, m * QUARTER : (m + 1) * QUARTER]
        planes = []
        for plane in range(2):
            value = jnp.zeros(ids.shape, jnp.float32)
            for level in range(LEVELS):
                value = jnp.where(ids == level, trans_ref[plane, level], value)
            planes.append(value)
        trans = jnp.concatenate(planes, axis=0).astype(jnp.bfloat16)
        pixels_ref[2 * ROWS * m : 2 * ROWS * (m + 1), :] = trans
        exact = trans.astype(jnp.float32)
        for tile in range(QUARTER // 128):
            total = total + exact[:, 128 * tile : 128 * tile + 128]
    table_copy.wait()
    product = jnp.dot(pixels_ref[...], table_ref[...], preferred_element_type=jnp.float32)
    cosines = [product[2 * ROWS * m : 2 * ROWS * (m + 1), :HALF] for m in range(4)]
    sines = [product[2 * ROWS * m : 2 * ROWS * (m + 1), HALF:] for m in range(4)]
    turns = lane_ids((2 * ROWS, HALF)) % 4
    zero = jnp.zeros((2 * ROWS, HALF), jnp.float32)

    def quarter(value, first):
        return jnp.where(turns == first, value, jnp.where(turns == first + 2, -value, zero))

    odd = turns % 2 == 1
    cosine = cosines[0] + jnp.where(odd, -cosines[2], cosines[2])
    cosine = cosine + quarter(cosines[1] + cosines[3], 0) - quarter(sines[1] - sines[3], 1)
    sine = sines[0] + jnp.where(odd, -sines[2], sines[2])
    sine = sine + quarter(cosines[1] - cosines[3], 1) + quarter(sines[1] + sines[3], 0)
    weight_cos, weight_sin = edge_values(lane_ids((1, 128)) % 16)
    edge_cos = jnp.sum(total * weight_cos, axis=1, keepdims=True)
    edge_sin = jnp.sum(total * weight_sin, axis=1, keepdims=True)
    cos_real, cos_imag = cosine[:ROWS], cosine[ROWS:]
    sin_real, sin_imag = sine[:ROWS], sine[ROWS:]
    first = lane_ids((ROWS, HALF)) == 0
    low_real = jnp.where(first, edge_cos[:ROWS] - edge_sin[ROWS:], cos_real - sin_imag)
    low_imag = jnp.where(first, edge_cos[ROWS:] + edge_sin[:ROWS], cos_imag + sin_real)
    low = jnp.concatenate([low_real, low_imag], axis=1).astype(jnp.bfloat16)
    high = jnp.concatenate([cos_real + sin_imag, cos_imag - sin_real], axis=1).astype(jnp.bfloat16)
    sides = [
        jnp.dot(low, perm_ref[0], preferred_element_type=jnp.float32),
        jnp.dot(high, perm_ref[1], preferred_element_type=jnp.float32),
    ]
    group = lane_ids((16, 128)) // WIDE
    for y in range(4):
        for x in range(4):
            owner = y * 4 + x
            chunk = jnp.zeros((16, 128), jnp.float32)
            for g in range(4):
                q, side = g // 2, g % 2
                major = owner // 4 * 128
                piece = sides[side][16 * q : 16 * q + 16, major : major + 128]
                turn = (g - owner) % 4 * WIDE
                piece = pltpu.roll(piece, turn, 1) if turn else piece
                chunk = jnp.where(group == g, piece, chunk)
            value = chunk.astype(jnp.bfloat16)
            for plane_z in range(4):
                dest = plane_z // 2 * 32 + y * 8 + plane_z % 2 * 4 + x
                out_ref[16 * dest : 16 * dest + 16, :] = value


def columns_call(trans_table, mask_ids, table):
    vmem = pl.BlockSpec(memory_space=pltpu.VMEM)
    hbm = pl.BlockSpec(memory_space=pl.ANY)
    return pl.pallas_call(
        columns_kernel,
        out_shape=jax.ShapeDtypeStruct((DEVICES // 2 * 16, 128), jnp.bfloat16),
        in_specs=[pl.BlockSpec(memory_space=pltpu.SMEM), hbm, hbm],
        out_specs=vmem,
        scratch_shapes=[
            pltpu.VMEM((ROWS, NPIX), jnp.int32),
            pltpu.VMEM((QUARTER, PASS), jnp.bfloat16),
            pltpu.VMEM((8 * ROWS, QUARTER), jnp.bfloat16),
            pltpu.VMEM((2, PASS, PASS), jnp.bfloat16),
            pltpu.SemaphoreType.DMA((2,)),
        ],
        compiler_params=pltpu.CompilerParams(vmem_limit_bytes=56 * MIB),
        name="columns",
    )(trans_table, mask_ids, table)


def spectrum_kernel(core_ref, table_hbm, cols_ref, keep_ref, send_ref, table_ref, block_ref, sems):
    core = core_ref[0]
    copies = []
    for q in range(2):
        copies.append(pltpu.make_async_copy(table_hbm.at[core, q], table_ref.at[q], sems.at[q]))
        copies[q].start()
    columns = cols_ref[...].astype(jnp.float32)
    total = [columns[16 * k : 16 * k + 16] for k in range(DEVICES // 2)]
    while len(total) > 1:
        total = [a + b for a, b in zip(total[::2], total[1::2])]
    weight_cos, weight_sin = edge_values(lax.broadcasted_iota(jnp.int32, (16, 128), 0))
    edge_cos = jnp.sum(total[0] * weight_cos, axis=0, keepdims=True)
    edge_sin = jnp.sum(total[0] * weight_sin, axis=0, keepdims=True)

    def turn(value):
        is_real = lane_ids(value.shape) % WIDE < FREQS
        return jnp.where(is_real, pltpu.roll(value, 128 - FREQS, 1), -pltpu.roll(value, FREQS, 1))

    edges = jnp.concatenate([edge_cos, edge_sin, jnp.zeros((6, 128), jnp.float32)], axis=0)
    edges = edges + pltpu.roll(edges, 64, 1)
    edge = edges[0:1] - turn(edges)[1:2]
    source = lax.broadcasted_iota(jnp.int32, (HALF, HALF), 0)
    place = lax.broadcasted_iota(jnp.int32, (HALF, HALF), 1)
    perm = (source == (HALF - place) % HALF).astype(jnp.float32).astype(jnp.bfloat16)
    rows = DEVICES // 4 * 16
    both = jnp.concatenate([cols_ref[:rows, :], cols_ref[rows:, :]], axis=1)
    odd = lax.broadcasted_iota(jnp.int32, (PASS, 128), 0) % 2 == 1
    products = []
    for q in range(2):
        copies[q].wait()
        product = jnp.dot(table_ref[q], both, preferred_element_type=jnp.float32)
        products.append(product[:, :128] + jnp.where(odd, -product[:, 128:], product[:, 128:]))
    folded = jnp.where(lane_ids((PASS, 128)) < 64, products[0], products[1])
    folded = folded + pltpu.roll(folded, 64, 1)
    cosine, turned = folded[:HALF], turn(folded[HALF:])
    first = lax.broadcasted_iota(jnp.int32, cosine.shape, 0) == 0
    scale = 1.0 / (NPIX * NPIX)
    high = jnp.transpose((cosine + turned) * scale)[: 2 * WIDE]
    low = jnp.transpose(jnp.where(first, edge, cosine - turned) * scale)[: 2 * WIDE]
    pieces = []
    rest = low
    for _ in range(3):
        piece = rest.astype(jnp.bfloat16)
        rest = rest - piece.astype(jnp.float32)
        pieces.append(jnp.dot(piece, perm, preferred_element_type=jnp.float32))
    block_ref[:, :HALF] = pieces[0] + pieces[1] + pieces[2]
    block_ref[:, HALF:] = high
    keep_ref[...] = block_ref[pl.ds(pl.multiple_of(core * WIDE, WIDE), WIDE), :]
    send_ref[...] = block_ref[pl.ds(pl.multiple_of((1 - core) * WIDE, WIDE), WIDE), :]


def spectrum_call(core, table, cols):
    vmem = pl.BlockSpec(memory_space=pltpu.VMEM)
    part = jax.ShapeDtypeStruct((WIDE, PASS), jnp.float32)
    return pl.pallas_call(
        spectrum_kernel,
        out_shape=(part, part),
        in_specs=[pl.BlockSpec(memory_space=pltpu.SMEM), pl.BlockSpec(memory_space=pl.ANY), vmem],
        out_specs=(vmem, vmem),
        scratch_shapes=[
            pltpu.VMEM((2,) + table.shape[2:], jnp.bfloat16),
            pltpu.VMEM((2 * WIDE, PASS), jnp.float32),
            pltpu.SemaphoreType.DMA((2,)),
        ],
        compiler_params=pltpu.CompilerParams(vmem_limit_bytes=50 * MIB),
        name="spectrum",
    )(core, table, cols)


def spread_kernel(keep_ref, come_ref, out_ref):
    block = keep_ref[...] + come_ref[...]
    for dest in range(16):
        out_ref[dest * WIDE : (dest + 1) * WIDE, :] = block


def spread_call(keep, come):
    vmem = pl.BlockSpec(memory_space=pltpu.VMEM)
    return pl.pallas_call(
        spread_kernel,
        out_shape=jax.ShapeDtypeStruct((16 * WIDE, PASS), jnp.float32),
        in_specs=[vmem, vmem],
        out_specs=vmem,
        compiler_params=pltpu.CompilerParams(vmem_limit_bytes=6 * MIB),
        name="spread",
    )(keep, come)


def pack_kernel(shifts_ref, weights_ref, dose_ref, last_ref, first_ref, note_ref):
    def note(shape):
        lane = lane_ids(shape)
        shift_x, shift_y = shifts_ref[0, 0].astype(jnp.float32), shifts_ref[0, 1].astype(jnp.float32)
        return jnp.where(lane == 64, shift_x, jnp.where(lane == 65, shift_y, weights_ref[0]))

    lane = lane_ids((BRICK_ROWS, 128))
    middle = (lane >= 64) & (lane < 67)
    for z in range(Z):
        last_ref[z] = jnp.where(middle, note((BRICK_ROWS, 128)), dose_ref[z, :, BRICK_COLS - 128 :])
        first_ref[z] = jnp.where(middle, note((BRICK_ROWS, 128)), dose_ref[z, :, :128])
    note_ref[...] = note((8, 128))


def pack_call(shifts, weights, dose):
    vmem = pl.BlockSpec(memory_space=pltpu.VMEM)
    smem = pl.BlockSpec(memory_space=pltpu.SMEM)
    side = jax.ShapeDtypeStruct((Z, BRICK_ROWS, 128), jnp.float32)
    return pl.pallas_call(
        pack_kernel,
        out_shape=(side, side, jax.ShapeDtypeStruct((8, 128), jnp.float32)),
        in_specs=[smem, smem, vmem],
        out_specs=(vmem,) * 3,
        compiler_params=pltpu.CompilerParams(vmem_limit_bytes=6 * MIB),
        cost_estimate=pl.CostEstimate(flops=1_000_000, bytes_accessed=9_000_000, transcendentals=0),
        name="pack",
    )(shifts, weights, dose)


def edge_kernel(dose_ref, before_ref, after_ref, side_ref, last_ref, first_ref, near_ref):
    near_ref[...] = dose_ref[...]
    lane = lane_ids((BRICK_ROWS, 128))
    for z in range(Z):
        side = jnp.where(lane < 64, after_ref[z], before_ref[z])
        side_ref[z] = side
        last_ref[z, :, :BRICK_COLS] = dose_ref[z, BRICK_ROWS - 8 :, :]
        last_ref[z, :, BRICK_COLS:] = side[BRICK_ROWS - 8 :]
        first_ref[z, :, :BRICK_COLS] = dose_ref[z, :8, :]
        first_ref[z, :, BRICK_COLS:] = side[:8]


def edge_call(dose, before, after):
    vmem = pl.BlockSpec(memory_space=pltpu.VMEM)
    row = jax.ShapeDtypeStruct((Z, 8, EXT_COLS), jnp.float32)
    return pl.pallas_call(
        edge_kernel,
        out_shape=(
            jax.ShapeDtypeStruct((Z, BRICK_ROWS, 128), jnp.float32),
            row,
            row,
            jax.ShapeDtypeStruct(dose.shape, jnp.float32),
        ),
        in_specs=[vmem] * 3,
        out_specs=(vmem,) * 4,
        compiler_params=pltpu.CompilerParams(vmem_limit_bytes=6 * MIB),
        cost_estimate=pl.CostEstimate(flops=1_000_000, bytes_accessed=2_000_000, transcendentals=0),
        name="edge",
    )(dose, before, after)


def window_kernel(shifts_ref, pupil_ref, out_hbm, token_ref, out_ref, turned_ref, sems):
    blocks = pupil_ref.shape[1] // 128
    for plane in range(2):
        for i in range(blocks):
            for j in range(blocks):
                piece = pupil_ref[plane, 128 * i : 128 * i + 128, 128 * j : 128 * j + 128]
                turned_ref[plane, 128 * j : 128 * j + 128, 128 * i : 128 * i + 128] = jnp.transpose(piece)
    token_ref[...] = jnp.zeros_like(token_ref)
    lane = lane_ids((8, 128))
    row = lax.broadcasted_iota(jnp.int32, (8, 128), 0)
    zero = jnp.zeros((8, 128), jnp.float32)
    tiles, group, groups = PASS // 8, 13, 4
    edge = SHIFT * 2 // 8

    def source_step(s, carry):
        lift = SHIFT - shifts_ref[s, 1]
        shift = SHIFT - shifts_ref[s, 0]
        first, rest = lift // 8, lax.rem(lift, 8)
        rise = lax.rem(8 - rest, 8)
        turn = lax.rem(256 - shift, 128)
        keep_lane = lane < 128 - shift
        keep_row = row < 8 - rest
        begin = jnp.minimum(edge - first - jnp.where(rest > 0, 1, 0), tiles - group * groups)

        def clear(t, inner):
            for plane in range(2):
                for v in range(4):
                    out_ref[2 * s + plane, pl.ds(pl.multiple_of(t * 8, 8), 8), 128 * v : 128 * v + 128] = zero
            return inner

        lax.fori_loop(0, begin, clear, 0)
        lax.fori_loop(begin + group * groups, tiles, clear, 0)

        def block(t, inner):
            start = begin + t * group
            for plane in range(2):
                before = None
                for k in range(group + 1):
                    tile = jnp.minimum(start + k + first, PUPIL_TILES - 1)
                    base = pl.ds(pl.multiple_of(tile * 8, 8), 8)
                    turned = [zero] + [
                        pltpu.roll(turned_ref[plane, base, 128 * v : 128 * v + 128], turn, 1) for v in range(1, 5)
                    ]
                    cut = [jnp.where(keep_lane, turned[v], turned[v + 1]) for v in range(4)]
                    after = [pltpu.roll(c, rise, 0) for c in cut]
                    if before is not None:
                        place = pl.ds(pl.multiple_of((start + k - 1) * 8, 8), 8)
                        for v in range(4):
                            value = jnp.where(keep_row, before[v], after[v])
                            out_ref[2 * s + plane, place, 128 * v : 128 * v + 128] = value
                    before = after
            return inner

        lax.fori_loop(0, groups, block, 0)
        leave(s).start()
        return carry

    def leave(s):
        planes = pl.ds(2 * s, 2)
        return pltpu.make_async_copy(out_ref.at[planes], out_hbm.at[planes], sems.at[s])

    lax.fori_loop(0, SOURCES, source_step, 0)
    for s in range(SOURCES):
        leave(s).wait()


def window_call(shifts, pupil):
    vmem = pl.BlockSpec(memory_space=pltpu.VMEM)
    planes = 2 * SOURCES
    return pl.pallas_call(
        window_kernel,
        out_shape=(
            jax.ShapeDtypeStruct((3 * planes, PASS, PASS), jnp.float32),
            jax.ShapeDtypeStruct((8, 128), jnp.float32),
        ),
        in_specs=[pl.BlockSpec(memory_space=pltpu.SMEM), vmem],
        out_specs=(pl.BlockSpec(memory_space=pl.ANY), vmem),
        scratch_shapes=[
            pltpu.VMEM((planes, PASS, PASS), jnp.float32),
            pltpu.VMEM(pupil.shape, jnp.float32),
            pltpu.SemaphoreType.DMA((SOURCES,)),
        ],
        compiler_params=pltpu.CompilerParams(vmem_limit_bytes=44 * MIB),
        cost_estimate=pl.CostEstimate(flops=10_000_000, bytes_accessed=11_000_000, transcendentals=0),
        name="window",
    )(shifts, pupil)


def rowfield_half(s, spec_ref, window_ref, rows_ref, filt_ref):
    slot = s % 2

    def block(o, inner):
        base = pl.multiple_of(o * WIDE, WIDE)
        place = pl.ds(pl.multiple_of(o * FREQS, FREQS), FREQS)
        real = spec_ref[pl.ds(base, FREQS), :]
        imag = spec_ref[pl.ds(base + FREQS, FREQS), :]
        w_real = window_ref[2 * s, place, :]
        w_imag = window_ref[2 * s + 1, place, :]
        filt_ref[slot, place, :PASS] = (w_real * real - w_imag * imag).astype(jnp.bfloat16)
        filt_ref[slot, place, PASS:] = (w_real * imag + w_imag * real).astype(jnp.bfloat16)
        return inner

    lax.fori_loop(0, 16, block, 0, unroll=16)
    return lax.dot_general(
        rows_ref[...], filt_ref[slot], (((1,), (1,)), ((), ())), preferred_element_type=jnp.float32
    ).astype(jnp.bfloat16)


def own_kernel(
    where_ref, token_ref, own_ref, window_hbm, rows_hbm,
    field_ref, rows_ref, other_ref, window_ref, filt_ref, sems,
):
    core = where_ref[0]
    mine = pl.ds(pl.multiple_of(core * HALF, HALF), HALF)
    theirs = pl.ds(pl.multiple_of((1 - core) * HALF, HALF), HALF)
    rows_copy = pltpu.make_async_copy(rows_hbm.at[where_ref[1]], rows_ref, sems.at[0])
    rows_copy.start()
    copies = []
    for s in range(SOURCES):
        planes = pl.ds(2 * s, 2)
        copies.append(pltpu.make_async_copy(window_hbm.at[planes, mine], window_ref.at[planes], sems.at[1 + s]))
        copies[s].start()
    later = pltpu.make_async_copy(window_hbm.at[pl.ds(0, 2 * SOURCES), theirs], other_ref, sems.at[1 + SOURCES])
    later.start()
    rows_copy.wait()
    for s in range(SOURCES):
        if s % 2 == 0:
            copies[s].wait()
            copies[s + 1].wait()
        rowfield = rowfield_half(s, own_ref, window_ref, rows_ref, filt_ref)
        field_ref[s * TALL : (s + 1) * TALL, :HALF] = rowfield[:TALL]
        field_ref[s * TALL : (s + 1) * TALL, HALF:] = rowfield[TALL:]
    later.wait()


def own_call(where, token, own, window, rows):
    smem = pl.BlockSpec(memory_space=pltpu.SMEM)
    vmem = pl.BlockSpec(memory_space=pltpu.VMEM)
    hbm = pl.BlockSpec(memory_space=pl.ANY)
    half = (2 * SOURCES, HALF, PASS)
    return pl.pallas_call(
        own_kernel,
        out_shape=(
            jax.ShapeDtypeStruct((SOURCES * TALL, PASS), jnp.bfloat16),
            jax.ShapeDtypeStruct(rows.shape[1:], jnp.bfloat16),
            jax.ShapeDtypeStruct(half, jnp.float32),
        ),
        in_specs=[smem, hbm, vmem, hbm, hbm],
        out_specs=(vmem,) * 3,
        scratch_shapes=[
            pltpu.VMEM(half, jnp.float32),
            pltpu.VMEM((2, HALF, 2 * PASS), jnp.bfloat16),
            pltpu.SemaphoreType.DMA((2 + SOURCES,)),
        ],
        compiler_params=pltpu.CompilerParams(vmem_limit_bytes=36 * MIB),
        cost_estimate=pl.CostEstimate(flops=10_000_000, bytes_accessed=9_000_000, transcendentals=0),
        name="own_half",
    )(where, token, own, window, rows)


def resist_kernel(
    where_ref, weights_ref, quencher_ref, half_ref, other_ref, window_ref, rows_ref, cols_hbm,
    dose_ref, side_ref, above_ref, below_ref, acid_hbm, inhibitor_hbm,
    cols_ref, filt_ref, field_ref, a_ref, b_ref, p_ref, q_ref, sum_ref, acid_ref, inhibitor_ref, sems, out_sems,
):
    core = where_ref[0]
    cols_copies = []
    for k, (begin, count) in enumerate(((0, EARLY), (EARLY, COL_TILES - EARLY))):
        part = pl.ds(begin, count)
        cols_copies.append(pltpu.make_async_copy(cols_hbm.at[where_ref[2], part], cols_ref.at[part], sems.at[k]))
        cols_copies[k].start()
    mine = pl.multiple_of(core * HALF, HALF)
    theirs = pl.multiple_of((1 - core) * HALF, HALF)
    field_ref[:, pl.ds(mine, HALF)] = half_ref[:, :HALF]
    field_ref[:, pl.ds(PASS + mine, HALF)] = half_ref[:, HALF:]
    for s in range(SOURCES):
        rowfield = rowfield_half(s, other_ref, window_ref, rows_ref, filt_ref)
        field_ref[s * TALL : (s + 1) * TALL, pl.ds(theirs, HALF)] = rowfield[:TALL]
        field_ref[s * TALL : (s + 1) * TALL, pl.ds(PASS + theirs, HALF)] = rowfield[TALL:]
    cols_copies[0].wait()
    row_of = lax.broadcasted_iota(jnp.int32, (8, 128), 0)

    for b in range(COL_TILES):
        if b == EARLY:
            cols_copies[1].wait()
        field = jnp.dot(field_ref[...], cols_ref[b], preferred_element_type=jnp.float32)
        intensity = jnp.zeros((EXT_ROWS, 128), jnp.float32)
        for s in range(SOURCES):
            part = field[s * TALL : s * TALL + EXT_ROWS]
            real, imag = part[:, :128], part[:, 128:]
            intensity = intensity + weights_ref[s] * (real * real + imag * imag)
        lanes = slice(b * 128, b * 128 + 128)
        for z in range(Z):
            bottom = jnp.where(row_of < HALO, below_ref[z, :, lanes], above_ref[z, :, lanes])
            middle = dose_ref[z, :, lanes] if b < COL_TILES - 1 else side_ref[z]
            a_ref[z, :BRICK_ROWS, lanes] = QUENCH_RATE - QUENCH_RATE * jnp.exp(-middle * intensity[:BRICK_ROWS])
            a_ref[z, BRICK_ROWS:, lanes] = QUENCH_RATE - QUENCH_RATE * jnp.exp(-bottom * intensity[BRICK_ROWS:])

    tiles = EXT_ROWS // 8
    row_id = lax.broadcasted_iota(jnp.int32, (8, EXT_COLS), 0)
    quench = [QUENCH_RATE * quencher_ref[0], QUENCH_RATE * quencher_ref[1]]

    def neighbours(ref, z, t):
        here = ref[z, 8 * t : 8 * t + 8, :]
        up, down = (t - 1) % tiles, (t + 1) % tiles
        above = pltpu.roll(jnp.where(row_id == 7, ref[z, 8 * up : 8 * up + 8, :], here), 1, 0)
        below = pltpu.roll(jnp.where(row_id == 0, ref[z, 8 * down : 8 * down + 8, :], here), 7, 0)
        left = pltpu.roll(here, 1, 1)
        right = pltpu.roll(here, EXT_COLS - 1, 1)
        return here, (above + below) + (left + right)

    buffers = [(a_ref, b_ref), (b_ref, a_ref), (a_ref, b_ref), (b_ref, None)]
    quenches = [(None, p_ref), (p_ref, q_ref), (q_ref, p_ref), (p_ref, None)]
    copies = []
    for step in range(BAKE):
        old, new = buffers[step]
        q_old, q_new = quenches[step]
        for t in range(tiles if new is not None else BRICK_ROWS // 8):
            rows = slice(8 * t, 8 * t + 8)
            acid = [neighbours(old, z, t) for z in range(Z)]
            acid_z = acid[0][0] + acid[1][0]
            if q_old is None:
                quench_here = quench
                quench_sum = [4.0 * quench[z] for z in range(Z)]
            elif q_new is None:
                quench_here = [q_old[z, rows, :] for z in range(Z)]
            else:
                pairs = [neighbours(q_old, z, t) for z in range(Z)]
                quench_here = [pair[0] for pair in pairs]
                quench_sum = [pair[1] for pair in pairs]
            quench_z = quench_here[0] + quench_here[1]
            for z in range(Z):
                here, around = acid[z]
                reaction = here * quench_here[z]
                fresh = ((1.0 - 6.0 * DIFF_ACID) * here + DIFF_ACID * (around + acid_z)) - reaction
                if new is not None:
                    new[z, rows, :] = fresh
                else:
                    acid_ref[z, rows, :] = fresh[:, :BRICK_COLS] * (1.0 / QUENCH_RATE)
                if q_new is not None:
                    kept = (1.0 - 6.0 * DIFF_QUENCH) * quench_here[z]
                    q_new[z, rows, :] = (kept + DIFF_QUENCH * (quench_sum[z] + quench_z)) - reaction
                if t < BRICK_ROWS // 8:
                    if step == 0:
                        sum_ref[z, rows, :] = here[:, :BRICK_COLS]
                    elif new is not None:
                        sum_ref[z, rows, :] = sum_ref[z, rows, :] + here[:, :BRICK_COLS]
                    else:
                        total = sum_ref[z, rows, :] + here[:, :BRICK_COLS]
                        inhibitor_ref[z, rows, :] = jnp.exp((-CATALYSIS / QUENCH_RATE) * total)
            if new is None and t % 4 == 3:
                ready = pl.ds(8 * (t - 3), 32)
                for k, (near, far) in enumerate(((acid_ref, acid_hbm), (inhibitor_ref, inhibitor_hbm))):
                    copy = pltpu.make_async_copy(near.at[:, ready], far.at[:, ready], out_sems.at[t // 4, k])
                    copy.start()
                    copies.append(copy)
    for copy in copies:
        copy.wait()


def resist_call(where, weights, quencher, half, other, window, rows, cols, dose, side, above, below):
    smem = pl.BlockSpec(memory_space=pltpu.SMEM)
    vmem = pl.BlockSpec(memory_space=pltpu.VMEM)
    hbm = pl.BlockSpec(memory_space=pl.ANY)
    brick_shape = (Z, BRICK_ROWS, BRICK_COLS)
    out = jax.ShapeDtypeStruct(brick_shape, jnp.float32)
    brick = pltpu.VMEM((Z, EXT_ROWS, EXT_COLS), jnp.float32)
    near = pltpu.VMEM(brick_shape, jnp.float32)
    return pl.pallas_call(
        resist_kernel,
        out_shape=(out, out),
        in_specs=[smem] * 3 + [vmem] * 4 + [hbm] + [vmem] * 4,
        out_specs=(hbm, hbm),
        scratch_shapes=[
            pltpu.VMEM(cols.shape[1:], jnp.bfloat16),
            pltpu.VMEM((2, HALF, 2 * PASS), jnp.bfloat16),
            pltpu.VMEM((SOURCES * TALL, 2 * PASS), jnp.bfloat16),
            brick, brick, brick, brick,
            near, near, near,
            pltpu.SemaphoreType.DMA((2,)),
            pltpu.SemaphoreType.DMA((4, 2)),
        ],
        compiler_params=pltpu.CompilerParams(vmem_limit_bytes=46 * MIB),
        name="resist",
    )(where, weights, quencher, half, other, window, rows, cols, dose, side, above, below)


def ring(axes, step):
    size = lax.axis_size(axes)
    return [(i, (i + step) % size) for i in range(size)]


def body(mask_ids, trans_table, pupil, shifts, weights, dose, quencher):
    src_axes, tile_axes = ("zl", "c"), ("y", "zh", "x")
    core, src, tile = lax.axis_index("c"), lax.axis_index(src_axes), lax.axis_index(tile_axes)
    packed = columns_call(trans_table, mask_ids, jnp.asarray(forward_columns()))
    packed, shifts, weights, dose_late = lax.optimization_barrier((packed, shifts, weights, dose))
    cols = lax.all_to_all(packed, ("zl", "y", "zh", "x"), 0, 0, tiled=True)

    last, first, note = pack_call(shifts, weights, dose_late)
    cols, last, first, note = lax.optimization_barrier((cols, last, first, note))
    before = lax.ppermute(last, src_axes, ring(src_axes, 1))
    after = lax.ppermute(first, src_axes, ring(src_axes, -1))
    far = lax.ppermute(note, src_axes, ring(src_axes, 2))
    notes = [note[:1, 64:67], far[:1, 64:67], before[0, :1, 64:67], after[0, :1, 64:67]]
    sources = jnp.concatenate(notes, axis=0)
    all_shifts, all_weights = sources[:, :2].astype(jnp.int32), sources[:, 2]
    side, last, first, dose_near = edge_call(dose_late, before, after)
    above = lax.ppermute(last, tile_axes, ring(tile_axes, 1))
    below = lax.ppermute(first, tile_axes, ring(tile_axes, -1))
    where = jnp.stack([core, tile, src]).astype(jnp.int32)

    swap = [(0, 1), (1, 0)]
    core_ref = core.reshape(1).astype(jnp.int32)
    keep, send = spectrum_call(core_ref, jnp.asarray(forward_rows()), cols)
    block = spread_call(keep, lax.ppermute(send, "c", swap))
    own = lax.all_to_all(block, ("y", "x"), 0, 0, tiled=True)
    window, token = window_call(all_shifts, pupil)
    own, token, all_weights, side, above, below, where = lax.optimization_barrier(
        (own, token, all_weights, side, above, below, where)
    )
    other = lax.ppermute(own, "c", swap)
    half, row_table, window_other = own_call(where, token, own, window, jnp.asarray(inverse_rows(32)))
    return resist_call(
        where, all_weights, quencher, half, other, window_other, row_table,
        jnp.asarray(inverse_cols(4)), dose_near, side, above, below,
    )


def solution(mesh):
    parts = Mesh(mesh.devices.reshape(2, 2, 4, 2, 4), ALL)
    src, tile = ("zl", "c"), ("y", "zh", "x")
    inner = jax.shard_map(
        body,
        mesh=parts,
        in_specs=(
            P(ALL, None),
            P(),
            P(),
            P(src, None),
            P(src),
            P(None, tile, src),
            P(),
        ),
        out_specs=(P(None, tile, src), P(None, tile, src)),
        check_vma=False,
    )
    return inner
```

```python
import math

import jax
import jax.numpy as jnp
import numpy as np
from jax import lax
from jax.experimental import pallas as pl
from jax.experimental.pallas import tpu as pltpu
from jax.sharding import Mesh, PartitionSpec as P

NPIX = 4096
PASS = 512
SHIFT = 64
LEVELS = 4
SOURCES = 4
BAKE = 4
Z = 2
PUPIL_TILES = (PASS + 2 * SHIFT) // 8
DIFF_ACID = 0.12
DIFF_QUENCH = 0.04
QUENCH_RATE = 0.6
CATALYSIS = 0.4

DEVICES = 128
ROWS = NPIX // DEVICES
OWNERS = 32
FREQS = PASS // OWNERS
WIDE = 2 * FREQS
HALO = 4
TALL = 144
BRICK_ROWS = 128
BRICK_COLS = 1024
EXT_ROWS = BRICK_ROWS + 2 * HALO
EXT_COLS = BRICK_COLS + 128
COL_TILES = EXT_COLS // 128
EARLY = 2
ALL = ("zl", "c", "y", "zh", "x")
MIB = 1024 * 1024
QUARTER = NPIX // 4


def cos_sin(first, second):
    theta = (np.mod(first[:, None] * second[None, :], NPIX)).astype(np.float32)
    theta = (theta * np.float32(2.0 * math.pi / NPIX)).astype(np.float64)
    return np.cos(theta).astype(np.float32), np.sin(theta).astype(np.float32)


def bf16(table):
    return np.asarray(table).astype(jnp.bfloat16)


FREQ = np.arange(PASS, dtype=np.int64) - PASS // 2
HALF = PASS // 2


def forward_columns():
    return bf16(np.concatenate(cos_sin(np.arange(QUARTER), np.arange(HALF)), axis=1))


def forward_rows():
    order = np.arange(2 * QUARTER).reshape(2, DEVICES // 4, 2, 16).transpose(0, 2, 1, 3).reshape(2 * QUARTER)
    both = np.concatenate(cos_sin(np.arange(HALF), order), axis=0)
    table = both.reshape(PASS, 2, 2, QUARTER // 2).transpose(1, 2, 0, 3)
    return bf16(np.pad(table, ((0, 0), (0, 14), (0, 0), (0, 0))))


def edge_values(place):
    tables = [bf16(part)[0] for part in cos_sin(np.array([HALF]), np.arange(16))]
    results = []
    for table in tables:
        value = jnp.zeros(place.shape, jnp.float32)
        for k in range(16):
            value = jnp.where(place == k, float(table[k]), value)
        results.append(value)
    return results


def inverse_rows(tiles):
    blocks = []
    for tile in range(tiles):
        local = np.arange(TALL)
        local = np.where(local < BRICK_ROWS + HALO, local, local - EXT_ROWS)
        pixels = np.mod(tile * BRICK_ROWS + local, NPIX)
        cosine, sine = cos_sin(pixels, FREQ)
        upper = np.concatenate([cosine, -sine], axis=1)
        lower = np.concatenate([sine, cosine], axis=1)
        blocks.append(np.concatenate([upper, lower], axis=0))
    return bf16(np.stack(blocks))


def inverse_cols(sources):
    lanes = np.arange(EXT_COLS)
    local = np.where(lanes < BRICK_COLS + 64, lanes, lanes - EXT_COLS)
    blocks = []
    for source in range(sources):
        pixels = np.mod(source * BRICK_COLS + local, NPIX)
        cosine, sine = cos_sin(FREQ, pixels)
        planes = [table.reshape(PASS, COL_TILES, 1, 128) for table in (cosine, sine)]
        both = np.concatenate(planes, axis=2).reshape(PASS, COL_TILES, 256)
        blocks.append(both.transpose(1, 0, 2))
    return bf16(np.stack(blocks))


def lane_ids(shape):
    return lax.broadcasted_iota(jnp.int32, shape, len(shape) - 1)


def columns_kernel(trans_ref, ids_hbm, table_hbm, out_ref, ids_ref, table_ref, pixels_ref, perm_ref, sems):
    ids_copy = pltpu.make_async_copy(ids_hbm, ids_ref, sems.at[0])
    table_copy = pltpu.make_async_copy(table_hbm, table_ref, sems.at[1])
    ids_copy.start()
    table_copy.start()
    source = lax.broadcasted_iota(jnp.int32, (PASS, PASS), 0)
    lane = lax.broadcasted_iota(jnp.int32, (PASS, PASS), 1)
    plane, place = lane // FREQS % 2, lane // WIDE * FREQS + lane % FREQS
    perm_ref[0] = (source == plane * HALF + (HALF - place) % HALF).astype(jnp.float32).astype(jnp.bfloat16)
    perm_ref[1] = (source == plane * HALF + place).astype(jnp.float32).astype(jnp.bfloat16)
    ids_copy.wait()
    total = jnp.zeros((2 * ROWS, 128), jnp.float32)
    for m in range(4):
        ids = ids_ref[:, m * QUARTER : (m + 1) * QUARTER]
        planes = []
        for plane in range(2):
            value = jnp.zeros(ids.shape, jnp.float32)
            for level in range(LEVELS):
                value = jnp.where(ids == level, trans_ref[plane, level], value)
            planes.append(value)
        trans = jnp.concatenate(planes, axis=0).astype(jnp.bfloat16)
        pixels_ref[2 * ROWS * m : 2 * ROWS * (m + 1), :] = trans
        exact = trans.astype(jnp.float32)
        for tile in range(QUARTER // 128):
            total = total + exact[:, 128 * tile : 128 * tile + 128]
    table_copy.wait()
    product = jnp.dot(pixels_ref[...], table_ref[...], preferred_element_type=jnp.float32)
    cosines = [product[2 * ROWS * m : 2 * ROWS * (m + 1), :HALF] for m in range(4)]
    sines = [product[2 * ROWS * m : 2 * ROWS * (m + 1), HALF:] for m in range(4)]
    turns = lane_ids((2 * ROWS, HALF)) % 4
    zero = jnp.zeros((2 * ROWS, HALF), jnp.float32)

    def quarter(value, first):
        return jnp.where(turns == first, value, jnp.where(turns == first + 2, -value, zero))

    odd = turns % 2 == 1
    cosine = cosines[0] + jnp.where(odd, -cosines[2], cosines[2])
    cosine = cosine + quarter(cosines[1] + cosines[3], 0) - quarter(sines[1] - sines[3], 1)
    sine = sines[0] + jnp.where(odd, -sines[2], sines[2])
    sine = sine + quarter(cosines[1] - cosines[3], 1) + quarter(sines[1] + sines[3], 0)
    weight_cos, weight_sin = edge_values(lane_ids((1, 128)) % 16)
    edge_cos = jnp.sum(total * weight_cos, axis=1, keepdims=True)
    edge_sin = jnp.sum(total * weight_sin, axis=1, keepdims=True)
    cos_real, cos_imag = cosine[:ROWS], cosine[ROWS:]
    sin_real, sin_imag = sine[:ROWS], sine[ROWS:]
    first = lane_ids((ROWS, HALF)) == 0
    low_real = jnp.where(first, edge_cos[:ROWS] - edge_sin[ROWS:], cos_real - sin_imag)
    low_imag = jnp.where(first, edge_cos[ROWS:] + edge_sin[:ROWS], cos_imag + sin_real)
    low = jnp.concatenate([low_real, low_imag], axis=1).astype(jnp.bfloat16)
    high = jnp.concatenate([cos_real + sin_imag, cos_imag - sin_real], axis=1).astype(jnp.bfloat16)
    sides = [
        jnp.dot(low, perm_ref[0], preferred_element_type=jnp.float32),
        jnp.dot(high, perm_ref[1], preferred_element_type=jnp.float32),
    ]
    group = lane_ids((16, 128)) // WIDE
    for y in range(4):
        for x in range(4):
            owner = y * 4 + x
            chunk = jnp.zeros((16, 128), jnp.float32)
            for g in range(4):
                q, side = g // 2, g % 2
                major = owner // 4 * 128
                piece = sides[side][16 * q : 16 * q + 16, major : major + 128]
                turn = (g - owner) % 4 * WIDE
                piece = pltpu.roll(piece, turn, 1) if turn else piece
                chunk = jnp.where(group == g, piece, chunk)
            value = chunk.astype(jnp.bfloat16)
            for plane_z in range(4):
                dest = plane_z // 2 * 32 + y * 8 + plane_z % 2 * 4 + x
                out_ref[16 * dest : 16 * dest + 16, :] = value


def columns_call(trans_table, mask_ids, table):
    vmem = pl.BlockSpec(memory_space=pltpu.VMEM)
    hbm = pl.BlockSpec(memory_space=pl.ANY)
    return pl.pallas_call(
        columns_kernel,
        out_shape=jax.ShapeDtypeStruct((DEVICES // 2 * 16, 128), jnp.bfloat16),
        in_specs=[pl.BlockSpec(memory_space=pltpu.SMEM), hbm, hbm],
        out_specs=vmem,
        scratch_shapes=[
            pltpu.VMEM((ROWS, NPIX), jnp.int32),
            pltpu.VMEM((QUARTER, PASS), jnp.bfloat16),
            pltpu.VMEM((8 * ROWS, QUARTER), jnp.bfloat16),
            pltpu.VMEM((2, PASS, PASS), jnp.bfloat16),
            pltpu.SemaphoreType.DMA((2,)),
        ],
        compiler_params=pltpu.CompilerParams(vmem_limit_bytes=56 * MIB),
        name="columns",
    )(trans_table, mask_ids, table)


def spectrum_kernel(core_ref, table_hbm, cols_ref, keep_ref, send_ref, table_ref, block_ref, sems):
    core = core_ref[0]
    copies = []
    for q in range(2):
        copies.append(pltpu.make_async_copy(table_hbm.at[core, q], table_ref.at[q], sems.at[q]))
        copies[q].start()
    columns = cols_ref[...].astype(jnp.float32)
    total = [columns[16 * k : 16 * k + 16] for k in range(DEVICES // 2)]
    while len(total) > 1:
        total = [a + b for a, b in zip(total[::2], total[1::2])]
    weight_cos, weight_sin = edge_values(lax.broadcasted_iota(jnp.int32, (16, 128), 0))
    edge_cos = jnp.sum(total[0] * weight_cos, axis=0, keepdims=True)
    edge_sin = jnp.sum(total[0] * weight_sin, axis=0, keepdims=True)

    def turn(value):
        is_real = lane_ids(value.shape) % WIDE < FREQS
        return jnp.where(is_real, pltpu.roll(value, 128 - FREQS, 1), -pltpu.roll(value, FREQS, 1))

    edges = jnp.concatenate([edge_cos, edge_sin, jnp.zeros((6, 128), jnp.float32)], axis=0)
    edges = edges + pltpu.roll(edges, 64, 1)
    edge = edges[0:1] - turn(edges)[1:2]
    source = lax.broadcasted_iota(jnp.int32, (HALF, HALF), 0)
    place = lax.broadcasted_iota(jnp.int32, (HALF, HALF), 1)
    perm = (source == (HALF - place) % HALF).astype(jnp.float32).astype(jnp.bfloat16)
    rows = DEVICES // 4 * 16
    both = jnp.concatenate([cols_ref[:rows, :], cols_ref[rows:, :]], axis=1)
    odd = lax.broadcasted_iota(jnp.int32, (PASS, 128), 0) % 2 == 1
    products = []
    for q in range(2):
        copies[q].wait()
        product = jnp.dot(table_ref[q], both, preferred_element_type=jnp.float32)
        products.append(product[:, :128] + jnp.where(odd, -product[:, 128:], product[:, 128:]))
    folded = jnp.where(lane_ids((PASS, 128)) < 64, products[0], products[1])
    folded = folded + pltpu.roll(folded, 64, 1)
    cosine, turned = folded[:HALF], turn(folded[HALF:])
    first = lax.broadcasted_iota(jnp.int32, cosine.shape, 0) == 0
    scale = 1.0 / (NPIX * NPIX)
    high = jnp.transpose((cosine + turned) * scale)[: 2 * WIDE]
    low = jnp.transpose(jnp.where(first, edge, cosine - turned) * scale)[: 2 * WIDE]
    pieces = []
    rest = low
    for _ in range(3):
        piece = rest.astype(jnp.bfloat16)
        rest = rest - piece.astype(jnp.float32)
        pieces.append(jnp.dot(piece, perm, preferred_element_type=jnp.float32))
    block_ref[:, :HALF] = pieces[0] + pieces[1] + pieces[2]
    block_ref[:, HALF:] = high
    keep_ref[...] = block_ref[pl.ds(pl.multiple_of(core * WIDE, WIDE), WIDE), :]
    send_ref[...] = block_ref[pl.ds(pl.multiple_of((1 - core) * WIDE, WIDE), WIDE), :]


def spectrum_call(core, table, cols):
    vmem = pl.BlockSpec(memory_space=pltpu.VMEM)
    part = jax.ShapeDtypeStruct((WIDE, PASS), jnp.float32)
    return pl.pallas_call(
        spectrum_kernel,
        out_shape=(part, part),
        in_specs=[pl.BlockSpec(memory_space=pltpu.SMEM), pl.BlockSpec(memory_space=pl.ANY), vmem],
        out_specs=(vmem, vmem),
        scratch_shapes=[
            pltpu.VMEM((2,) + table.shape[2:], jnp.bfloat16),
            pltpu.VMEM((2 * WIDE, PASS), jnp.float32),
            pltpu.SemaphoreType.DMA((2,)),
        ],
        compiler_params=pltpu.CompilerParams(vmem_limit_bytes=50 * MIB),
        name="spectrum",
    )(core, table, cols)


def spread_kernel(keep_ref, come_ref, out_ref):
    block = keep_ref[...] + come_ref[...]
    for dest in range(16):
        out_ref[dest * WIDE : (dest + 1) * WIDE, :] = block


def spread_call(keep, come):
    vmem = pl.BlockSpec(memory_space=pltpu.VMEM)
    return pl.pallas_call(
        spread_kernel,
        out_shape=jax.ShapeDtypeStruct((16 * WIDE, PASS), jnp.float32),
        in_specs=[vmem, vmem],
        out_specs=vmem,
        compiler_params=pltpu.CompilerParams(vmem_limit_bytes=6 * MIB),
        name="spread",
    )(keep, come)


def pack_kernel(shifts_ref, weights_ref, dose_ref, last_ref, first_ref, note_ref):
    def note(shape):
        lane = lane_ids(shape)
        shift_x, shift_y = shifts_ref[0, 0].astype(jnp.float32), shifts_ref[0, 1].astype(jnp.float32)
        return jnp.where(lane == 64, shift_x, jnp.where(lane == 65, shift_y, weights_ref[0]))

    lane = lane_ids((BRICK_ROWS, 128))
    middle = (lane >= 64) & (lane < 67)
    for z in range(Z):
        last_ref[z] = jnp.where(middle, note((BRICK_ROWS, 128)), dose_ref[z, :, BRICK_COLS - 128 :])
        first_ref[z] = jnp.where(middle, note((BRICK_ROWS, 128)), dose_ref[z, :, :128])
    note_ref[...] = note((8, 128))


def pack_call(shifts, weights, dose):
    vmem = pl.BlockSpec(memory_space=pltpu.VMEM)
    smem = pl.BlockSpec(memory_space=pltpu.SMEM)
    side = jax.ShapeDtypeStruct((Z, BRICK_ROWS, 128), jnp.float32)
    return pl.pallas_call(
        pack_kernel,
        out_shape=(side, side, jax.ShapeDtypeStruct((8, 128), jnp.float32)),
        in_specs=[smem, smem, vmem],
        out_specs=(vmem,) * 3,
        compiler_params=pltpu.CompilerParams(vmem_limit_bytes=6 * MIB),
        cost_estimate=pl.CostEstimate(flops=1_000_000, bytes_accessed=9_000_000, transcendentals=0),
        name="pack",
    )(shifts, weights, dose)


def edge_kernel(dose_ref, before_ref, after_ref, side_ref, last_ref, first_ref, near_ref):
    near_ref[...] = dose_ref[...]
    lane = lane_ids((BRICK_ROWS, 128))
    for z in range(Z):
        side = jnp.where(lane < 64, after_ref[z], before_ref[z])
        side_ref[z] = side
        last_ref[z, :, :BRICK_COLS] = dose_ref[z, BRICK_ROWS - 8 :, :]
        last_ref[z, :, BRICK_COLS:] = side[BRICK_ROWS - 8 :]
        first_ref[z, :, :BRICK_COLS] = dose_ref[z, :8, :]
        first_ref[z, :, BRICK_COLS:] = side[:8]


def edge_call(dose, before, after):
    vmem = pl.BlockSpec(memory_space=pltpu.VMEM)
    row = jax.ShapeDtypeStruct((Z, 8, EXT_COLS), jnp.float32)
    return pl.pallas_call(
        edge_kernel,
        out_shape=(
            jax.ShapeDtypeStruct((Z, BRICK_ROWS, 128), jnp.float32),
            row,
            row,
            jax.ShapeDtypeStruct(dose.shape, jnp.float32),
        ),
        in_specs=[vmem] * 3,
        out_specs=(vmem,) * 4,
        compiler_params=pltpu.CompilerParams(vmem_limit_bytes=6 * MIB),
        cost_estimate=pl.CostEstimate(flops=1_000_000, bytes_accessed=2_000_000, transcendentals=0),
        name="edge",
    )(dose, before, after)


def window_kernel(shifts_ref, pupil_ref, out_hbm, token_ref, out_ref, turned_ref, sems):
    blocks = pupil_ref.shape[1] // 128
    for plane in range(2):
        for i in range(blocks):
            for j in range(blocks):
                piece = pupil_ref[plane, 128 * i : 128 * i + 128, 128 * j : 128 * j + 128]
                turned_ref[plane, 128 * j : 128 * j + 128, 128 * i : 128 * i + 128] = jnp.transpose(piece)
    token_ref[...] = jnp.zeros_like(token_ref)
    lane = lane_ids((8, 128))
    row = lax.broadcasted_iota(jnp.int32, (8, 128), 0)
    zero = jnp.zeros((8, 128), jnp.float32)
    tiles, group, groups = PASS // 8, 13, 4
    edge = SHIFT * 2 // 8

    def source_step(s, carry):
        lift = SHIFT - shifts_ref[s, 1]
        shift = SHIFT - shifts_ref[s, 0]
        first, rest = lift // 8, lax.rem(lift, 8)
        rise = lax.rem(8 - rest, 8)
        turn = lax.rem(256 - shift, 128)
        keep_lane = lane < 128 - shift
        keep_row = row < 8 - rest
        begin = jnp.minimum(edge - first - jnp.where(rest > 0, 1, 0), tiles - group * groups)

        def clear(t, inner):
            for plane in range(2):
                for v in range(4):
                    out_ref[2 * s + plane, pl.ds(pl.multiple_of(t * 8, 8), 8), 128 * v : 128 * v + 128] = zero
            return inner

        lax.fori_loop(0, begin, clear, 0)
        lax.fori_loop(begin + group * groups, tiles, clear, 0)

        def block(t, inner):
            start = begin + t * group
            for plane in range(2):
                before = None
                for k in range(group + 1):
                    tile = jnp.minimum(start + k + first, PUPIL_TILES - 1)
                    base = pl.ds(pl.multiple_of(tile * 8, 8), 8)
                    turned = [zero] + [
                        pltpu.roll(turned_ref[plane, base, 128 * v : 128 * v + 128], turn, 1) for v in range(1, 5)
                    ]
                    cut = [jnp.where(keep_lane, turned[v], turned[v + 1]) for v in range(4)]
                    after = [pltpu.roll(c, rise, 0) for c in cut]
                    if before is not None:
                        place = pl.ds(pl.multiple_of((start + k - 1) * 8, 8), 8)
                        for v in range(4):
                            value = jnp.where(keep_row, before[v], after[v])
                            out_ref[2 * s + plane, place, 128 * v : 128 * v + 128] = value
                    before = after
            return inner

        lax.fori_loop(0, groups, block, 0)
        leave(s).start()
        return carry

    def leave(s):
        planes = pl.ds(2 * s, 2)
        return pltpu.make_async_copy(out_ref.at[planes], out_hbm.at[planes], sems.at[s])

    lax.fori_loop(0, SOURCES, source_step, 0)
    for s in range(SOURCES):
        leave(s).wait()


def window_call(shifts, pupil):
    vmem = pl.BlockSpec(memory_space=pltpu.VMEM)
    planes = 2 * SOURCES
    return pl.pallas_call(
        window_kernel,
        out_shape=(
            jax.ShapeDtypeStruct((3 * planes, PASS, PASS), jnp.float32),
            jax.ShapeDtypeStruct((8, 128), jnp.float32),
        ),
        in_specs=[pl.BlockSpec(memory_space=pltpu.SMEM), vmem],
        out_specs=(pl.BlockSpec(memory_space=pl.ANY), vmem),
        scratch_shapes=[
            pltpu.VMEM((planes, PASS, PASS), jnp.float32),
            pltpu.VMEM(pupil.shape, jnp.float32),
            pltpu.SemaphoreType.DMA((SOURCES,)),
        ],
        compiler_params=pltpu.CompilerParams(vmem_limit_bytes=44 * MIB),
        cost_estimate=pl.CostEstimate(flops=10_000_000, bytes_accessed=11_000_000, transcendentals=0),
        name="window",
    )(shifts, pupil)


def rowfield_half(s, spec_ref, window_ref, rows_ref, filt_ref):
    slot = s % 2

    def block(o, inner):
        base = pl.multiple_of(o * WIDE, WIDE)
        place = pl.ds(pl.multiple_of(o * FREQS, FREQS), FREQS)
        real = spec_ref[pl.ds(base, FREQS), :]
        imag = spec_ref[pl.ds(base + FREQS, FREQS), :]
        w_real = window_ref[2 * s, place, :]
        w_imag = window_ref[2 * s + 1, place, :]
        filt_ref[slot, place, :PASS] = (w_real * real - w_imag * imag).astype(jnp.bfloat16)
        filt_ref[slot, place, PASS:] = (w_real * imag + w_imag * real).astype(jnp.bfloat16)
        return inner

    lax.fori_loop(0, 16, block, 0, unroll=16)
    return lax.dot_general(
        rows_ref[...], filt_ref[slot], (((1,), (1,)), ((), ())), preferred_element_type=jnp.float32
    ).astype(jnp.bfloat16)


def own_kernel(
    where_ref, token_ref, own_ref, window_hbm, rows_hbm,
    field_ref, rows_ref, other_ref, window_ref, filt_ref, sems,
):
    core = where_ref[0]
    mine = pl.ds(pl.multiple_of(core * HALF, HALF), HALF)
    theirs = pl.ds(pl.multiple_of((1 - core) * HALF, HALF), HALF)
    rows_copy = pltpu.make_async_copy(rows_hbm.at[where_ref[1]], rows_ref, sems.at[0])
    rows_copy.start()
    copies = []
    for s in range(SOURCES):
        planes = pl.ds(2 * s, 2)
        copies.append(pltpu.make_async_copy(window_hbm.at[planes, mine], window_ref.at[planes], sems.at[1 + s]))
        copies[s].start()
    later = pltpu.make_async_copy(window_hbm.at[pl.ds(0, 2 * SOURCES), theirs], other_ref, sems.at[1 + SOURCES])
    later.start()
    rows_copy.wait()
    for s in range(SOURCES):
        if s % 2 == 0:
            copies[s].wait()
            copies[s + 1].wait()
        rowfield = rowfield_half(s, own_ref, window_ref, rows_ref, filt_ref)
        field_ref[s * TALL : (s + 1) * TALL, :HALF] = rowfield[:TALL]
        field_ref[s * TALL : (s + 1) * TALL, HALF:] = rowfield[TALL:]
    later.wait()


def own_call(where, token, own, window, rows):
    smem = pl.BlockSpec(memory_space=pltpu.SMEM)
    vmem = pl.BlockSpec(memory_space=pltpu.VMEM)
    hbm = pl.BlockSpec(memory_space=pl.ANY)
    half = (2 * SOURCES, HALF, PASS)
    return pl.pallas_call(
        own_kernel,
        out_shape=(
            jax.ShapeDtypeStruct((SOURCES * TALL, PASS), jnp.bfloat16),
            jax.ShapeDtypeStruct(rows.shape[1:], jnp.bfloat16),
            jax.ShapeDtypeStruct(half, jnp.float32),
        ),
        in_specs=[smem, hbm, vmem, hbm, hbm],
        out_specs=(vmem,) * 3,
        scratch_shapes=[
            pltpu.VMEM(half, jnp.float32),
            pltpu.VMEM((2, HALF, 2 * PASS), jnp.bfloat16),
            pltpu.SemaphoreType.DMA((2 + SOURCES,)),
        ],
        compiler_params=pltpu.CompilerParams(vmem_limit_bytes=36 * MIB),
        cost_estimate=pl.CostEstimate(flops=10_000_000, bytes_accessed=9_000_000, transcendentals=0),
        name="own_half",
    )(where, token, own, window, rows)


def resist_kernel(
    where_ref, weights_ref, quencher_ref, half_ref, other_ref, window_ref, rows_ref, cols_hbm,
    dose_ref, side_ref, above_ref, below_ref, acid_hbm, inhibitor_hbm,
    cols_ref, filt_ref, field_ref, a_ref, b_ref, p_ref, q_ref, sum_ref, acid_ref, inhibitor_ref, sems, out_sems,
):
    core = where_ref[0]
    cols_copies = []
    for k, (begin, count) in enumerate(((0, EARLY), (EARLY, COL_TILES - EARLY))):
        part = pl.ds(begin, count)
        cols_copies.append(pltpu.make_async_copy(cols_hbm.at[where_ref[2], part], cols_ref.at[part], sems.at[k]))
        cols_copies[k].start()
    mine = pl.multiple_of(core * HALF, HALF)
    theirs = pl.multiple_of((1 - core) * HALF, HALF)
    field_ref[:, pl.ds(mine, HALF)] = half_ref[:, :HALF]
    field_ref[:, pl.ds(PASS + mine, HALF)] = half_ref[:, HALF:]
    for s in range(SOURCES):
        rowfield = rowfield_half(s, other_ref, window_ref, rows_ref, filt_ref)
        field_ref[s * TALL : (s + 1) * TALL, pl.ds(theirs, HALF)] = rowfield[:TALL]
        field_ref[s * TALL : (s + 1) * TALL, pl.ds(PASS + theirs, HALF)] = rowfield[TALL:]
    cols_copies[0].wait()
    row_of = lax.broadcasted_iota(jnp.int32, (8, 128), 0)

    for b in range(COL_TILES):
        if b == EARLY:
            cols_copies[1].wait()
        upper = jnp.dot(field_ref[:, :PASS], cols_ref[b], preferred_element_type=jnp.float32)
        lower = jnp.dot(field_ref[:, PASS:], cols_ref[b], preferred_element_type=jnp.float32)
        intensity = jnp.zeros((EXT_ROWS, 128), jnp.float32)
        for s in range(SOURCES):
            rows = slice(s * TALL, s * TALL + EXT_ROWS)
            real = upper[rows, :128] - lower[rows, 128:]
            imag = upper[rows, 128:] + lower[rows, :128]
            intensity = intensity + weights_ref[s] * (real * real + imag * imag)
        lanes = slice(b * 128, b * 128 + 128)
        for z in range(Z):
            bottom = jnp.where(row_of < HALO, below_ref[z, :, lanes], above_ref[z, :, lanes])
            middle = dose_ref[z, :, lanes] if b < COL_TILES - 1 else side_ref[z]
            a_ref[z, :BRICK_ROWS, lanes] = QUENCH_RATE - QUENCH_RATE * jnp.exp(-middle * intensity[:BRICK_ROWS])
            a_ref[z, BRICK_ROWS:, lanes] = QUENCH_RATE - QUENCH_RATE * jnp.exp(-bottom * intensity[BRICK_ROWS:])

    tiles = EXT_ROWS // 8
    row_id = lax.broadcasted_iota(jnp.int32, (8, EXT_COLS), 0)
    quench = [QUENCH_RATE * quencher_ref[0], QUENCH_RATE * quencher_ref[1]]

    def neighbours(ref, z, t):
        here = ref[z, 8 * t : 8 * t + 8, :]
        up, down = (t - 1) % tiles, (t + 1) % tiles
        above = pltpu.roll(jnp.where(row_id == 7, ref[z, 8 * up : 8 * up + 8, :], here), 1, 0)
        below = pltpu.roll(jnp.where(row_id == 0, ref[z, 8 * down : 8 * down + 8, :], here), 7, 0)
        left = pltpu.roll(here, 1, 1)
        right = pltpu.roll(here, EXT_COLS - 1, 1)
        return here, (above + below) + (left + right)

    buffers = [(a_ref, b_ref), (b_ref, a_ref), (a_ref, b_ref), (b_ref, None)]
    quenches = [(None, p_ref), (p_ref, q_ref), (q_ref, p_ref), (p_ref, None)]
    copies = []
    for step in range(BAKE):
        old, new = buffers[step]
        q_old, q_new = quenches[step]
        for t in range(tiles if new is not None else BRICK_ROWS // 8):
            rows = slice(8 * t, 8 * t + 8)
            acid = [neighbours(old, z, t) for z in range(Z)]
            acid_z = acid[0][0] + acid[1][0]
            if q_old is None:
                quench_here = quench
                quench_sum = [4.0 * quench[z] for z in range(Z)]
            elif q_new is None:
                quench_here = [q_old[z, rows, :] for z in range(Z)]
            else:
                pairs = [neighbours(q_old, z, t) for z in range(Z)]
                quench_here = [pair[0] for pair in pairs]
                quench_sum = [pair[1] for pair in pairs]
            quench_z = quench_here[0] + quench_here[1]
            for z in range(Z):
                here, around = acid[z]
                reaction = here * quench_here[z]
                fresh = ((1.0 - 6.0 * DIFF_ACID) * here + DIFF_ACID * (around + acid_z)) - reaction
                if new is not None:
                    new[z, rows, :] = fresh
                else:
                    acid_ref[z, rows, :] = fresh[:, :BRICK_COLS] * (1.0 / QUENCH_RATE)
                if q_new is not None:
                    kept = (1.0 - 6.0 * DIFF_QUENCH) * quench_here[z]
                    q_new[z, rows, :] = (kept + DIFF_QUENCH * (quench_sum[z] + quench_z)) - reaction
                if t < BRICK_ROWS // 8:
                    if step == 0:
                        sum_ref[z, rows, :] = here[:, :BRICK_COLS]
                    elif new is not None:
                        sum_ref[z, rows, :] = sum_ref[z, rows, :] + here[:, :BRICK_COLS]
                    else:
                        total = sum_ref[z, rows, :] + here[:, :BRICK_COLS]
                        inhibitor_ref[z, rows, :] = jnp.exp((-CATALYSIS / QUENCH_RATE) * total)
            if new is None and t % 4 == 3:
                ready = pl.ds(8 * (t - 3), 32)
                for k, (near, far) in enumerate(((acid_ref, acid_hbm), (inhibitor_ref, inhibitor_hbm))):
                    copy = pltpu.make_async_copy(near.at[:, ready], far.at[:, ready], out_sems.at[t // 4, k])
                    copy.start()
                    copies.append(copy)
    for copy in copies:
        copy.wait()


def resist_call(where, weights, quencher, half, other, window, rows, cols, dose, side, above, below):
    smem = pl.BlockSpec(memory_space=pltpu.SMEM)
    vmem = pl.BlockSpec(memory_space=pltpu.VMEM)
    hbm = pl.BlockSpec(memory_space=pl.ANY)
    brick_shape = (Z, BRICK_ROWS, BRICK_COLS)
    out = jax.ShapeDtypeStruct(brick_shape, jnp.float32)
    brick = pltpu.VMEM((Z, EXT_ROWS, EXT_COLS), jnp.float32)
    near = pltpu.VMEM(brick_shape, jnp.float32)
    return pl.pallas_call(
        resist_kernel,
        out_shape=(out, out),
        in_specs=[smem] * 3 + [vmem] * 4 + [hbm] + [vmem] * 4,
        out_specs=(hbm, hbm),
        scratch_shapes=[
            pltpu.VMEM(cols.shape[1:], jnp.bfloat16),
            pltpu.VMEM((2, HALF, 2 * PASS), jnp.bfloat16),
            pltpu.VMEM((SOURCES * TALL, 2 * PASS), jnp.bfloat16),
            brick, brick, brick, brick,
            near, near, near,
            pltpu.SemaphoreType.DMA((2,)),
            pltpu.SemaphoreType.DMA((4, 2)),
        ],
        compiler_params=pltpu.CompilerParams(vmem_limit_bytes=46 * MIB),
        name="resist",
    )(where, weights, quencher, half, other, window, rows, cols, dose, side, above, below)


def ring(axes, step):
    size = lax.axis_size(axes)
    return [(i, (i + step) % size) for i in range(size)]


def body(mask_ids, trans_table, pupil, shifts, weights, dose, quencher):
    src_axes, tile_axes = ("zl", "c"), ("y", "zh", "x")
    core, src, tile = lax.axis_index("c"), lax.axis_index(src_axes), lax.axis_index(tile_axes)
    packed = columns_call(trans_table, mask_ids, jnp.asarray(forward_columns()))
    packed, shifts, weights, dose_late = lax.optimization_barrier((packed, shifts, weights, dose))
    cols = lax.all_to_all(packed, ("zl", "y", "zh", "x"), 0, 0, tiled=True)

    last, first, note = pack_call(shifts, weights, dose_late)
    cols, last, first, note = lax.optimization_barrier((cols, last, first, note))
    before = lax.ppermute(last, src_axes, ring(src_axes, 1))
    after = lax.ppermute(first, src_axes, ring(src_axes, -1))
    far = lax.ppermute(note, src_axes, ring(src_axes, 2))
    notes = [note[:1, 64:67], far[:1, 64:67], before[0, :1, 64:67], after[0, :1, 64:67]]
    sources = jnp.concatenate(notes, axis=0)
    all_shifts, all_weights = sources[:, :2].astype(jnp.int32), sources[:, 2]
    side, last, first, dose_near = edge_call(dose_late, before, after)
    above = lax.ppermute(last, tile_axes, ring(tile_axes, 1))
    below = lax.ppermute(first, tile_axes, ring(tile_axes, -1))
    where = jnp.stack([core, tile, src]).astype(jnp.int32)

    swap = [(0, 1), (1, 0)]
    core_ref = core.reshape(1).astype(jnp.int32)
    keep, send = spectrum_call(core_ref, jnp.asarray(forward_rows()), cols)
    block = spread_call(keep, lax.ppermute(send, "c", swap))
    own = lax.all_to_all(block, ("y", "x"), 0, 0, tiled=True)
    window, token = window_call(all_shifts, pupil)
    own, token, all_weights, side, above, below, where = lax.optimization_barrier(
        (own, token, all_weights, side, above, below, where)
    )
    other = lax.ppermute(own, "c", swap)
    half, row_table, window_other = own_call(where, token, own, window, jnp.asarray(inverse_rows(32)))
    return resist_call(
        where, all_weights, quencher, half, other, window_other, row_table,
        jnp.asarray(inverse_cols(4)), dose_near, side, above, below,
    )


def solution(mesh):
    parts = Mesh(mesh.devices.reshape(2, 2, 4, 2, 4), ALL)
    src, tile = ("zl", "c"), ("y", "zh", "x")
    inner = jax.shard_map(
        body,
        mesh=parts,
        in_specs=(
            P(ALL, None),
            P(),
            P(),
            P(src, None),
            P(src),
            P(None, tile, src),
            P(),
        ),
        out_specs=(P(None, tile, src), P(None, tile, src)),
        check_vma=False,
    )
    return inner
```
